32 devices in a mesh: grp: 4 (over y, x), rep: 8 (over z, core).
Axes of the slice: x: 2, y: 2, z: 4, core: 2. Of those that a mesh axis runs over, the one named last changes fastest.
Arguments:
- forward: float32 [2, 2097152], P(None, ('grp', 'rep')), may hold values from -40 to 40
- adjoint: float32 [2, 2097152], P(None, ('grp', 'rep')), may hold values from -40 to 40
- edges: int32 [60, 2], replicated, may hold values from 0 to 39, as said below
- weights: int32 [60], replicated, may hold values from 1 to 9
- layout: int32 [40], replicated, may hold values from 0 to 39, each once
- slab_bits: int32 [40], replicated, may hold values from 0 to 1
- angles: float32 [4], replicated, may hold values from 0.6 to 1
Outputs:
- forward_out: float32 [2, 2097152], P(None, ('grp', 'rep'))
- adjoint_out: float32 [2, 2097152], P(None, ('grp', 'rep'))
- grads: float32 [4], replicated
The draws below stay inside these ranges and needn't reach their ends.
Inputs may be any that keep to these rules, and one draw needn't show every extreme that they name: `edges`: the two end nodes of an edge differ.
All inputs are finite; a program needn't handle non-finite values.
Results may differ from the reference program's by a relative error of at most 0.0003.
Values sent between devices are 32-bit elements; how exact they have to be, the bound alone decides.
No kernel may reach another device: no remote copies, remote signals or barrier semaphores. Data moves between devices by JAX's collectives and lax.ppermute only.
A program may use at most 64 MiB of HBM per device.

```python
import jax
import jax.numpy as jnp
from jax import lax

NODES = 40
EDGES = 60
LAYERS = 2
AMPS = 2097152


def shared_state(key, tilt_amount):
    base_draw = jax.random.truncated_normal(key, -6.0, 6.0, (2, AMPS), jnp.float32)
    position = jnp.arange(AMPS, dtype=jnp.float32) / AMPS
    scale_ramp = jnp.sqrt(1.0 + tilt_amount * position)
    return base_draw * scale_ramp[None, :]


def draw_forward(key, part):
    state_pair = shared_state(key, 2.0)
    return state_pair


def draw_adjoint(key, part):
    state_pair = shared_state(key, 2.0)
    key = jax.random.fold_in(key, 9)
    key_real, key_imag, key_noise = jax.random.split(key, 3)
    real_mix = jax.random.uniform(key_real, (AMPS,), jnp.float32, -1.0, 1.0)
    imag_mix = jax.random.uniform(key_imag, (AMPS,), jnp.float32, 0.05, 0.3)
    noise_pair = 0.5 * jax.random.truncated_normal(key_noise, -6.0, 6.0, (2, AMPS), jnp.float32)
    top_flip = jnp.flip(state_pair.reshape(2, 2, AMPS // 2), 1).reshape(2, AMPS)
    low_flip = jnp.flip(state_pair.reshape(2, AMPS // 2, 2), 2).reshape(2, AMPS)
    flipped = 0.25 * (top_flip + low_flip)
    real_out = state_pair[0] * real_mix - state_pair[1] * imag_mix - flipped[1] + noise_pair[0]
    imag_out = state_pair[0] * imag_mix + state_pair[1] * real_mix + flipped[0] + noise_pair[1]
    return jnp.stack([real_out, imag_out])


def draw_edges(key, part):
    key = jax.random.fold_in(key, 11)
    key_first, key_step = jax.random.split(key)
    first_end = jax.random.randint(key_first, (EDGES,), 0, NODES, jnp.int32)
    stride = jax.random.randint(key_step, (EDGES,), 1, NODES, jnp.int32)
    second = (first_end + stride) % NODES
    return jnp.stack([first_end, second], axis=1)


def set_ends(entries, key, least, top_value):
    place = [jax.random.randint(jax.random.fold_in(key, axis), (), 0, length) for axis, length in enumerate(entries.shape)]
    longest = entries.shape.index(max(entries.shape))
    neighbour = place[:longest] + [(place[longest] + 1) % entries.shape[longest]] + place[longest + 1:]
    return entries.at[tuple(place)].set(least).at[tuple(neighbour)].set(top_value)


def setup_inputs(seed: int = 0) -> dict:
    seeds = jax.random.split(jax.random.key(seed), 8)
    return {
        "forward": draw_forward(jax.random.fold_in(seeds[7], 71), 0),
        "adjoint": draw_adjoint(jax.random.fold_in(seeds[7], 71), 0),
        "edges": draw_edges(jax.random.fold_in(seeds[7], 71), 0),
        "weights": set_ends(jax.random.randint(seeds[3], (EDGES,), 1, 10), jax.random.fold_in(seeds[3], 1), 1, 9).astype(jnp.int32),
        "layout": jax.random.permutation(seeds[4], NODES).astype(jnp.int32),
        "slab_bits": set_ends(jax.random.randint(seeds[5], (NODES,), 0, 2), jax.random.fold_in(seeds[5], 1), 0, 1).astype(jnp.int32),
        "angles": jnp.clip(jax.random.uniform(seeds[6], (2 * LAYERS,), jnp.float32, 0.6, 1.0), 0.6, 1.0),
    }


def coupling(edges, weights):
    node_ids = jnp.arange(NODES, dtype=jnp.int32)
    first_end = (edges[:, 0:1] == node_ids[None, :]).astype(jnp.float32)
    second = (edges[:, 1:2] == node_ids[None, :]).astype(jnp.float32)
    weighted = first_end * weights.astype(jnp.float32)[:, None]
    matrix = jnp.dot(weighted.T, second, preferred_element_type=jnp.float32)
    return matrix + matrix.T, jnp.sum(weights.astype(jnp.float32))


def cost_field(edges, weights, layout, slab_bits, qubit_count):
    matrix, weight_total = coupling(edges, weights)
    block_len = min(AMPS, 65536)
    shifts = jnp.minimum(layout, qubit_count - 1).astype(jnp.int32)
    inside = layout < qubit_count

    def one_block(block_idx):
        offsets = block_idx * block_len + jnp.arange(block_len, dtype=jnp.int32)
        spin_bits = (offsets[:, None] >> shifts[None, :]) & 1
        spin_bits = jnp.where(inside[None, :], spin_bits, slab_bits[None, :])
        spin_vals = (1 - 2 * spin_bits).astype(jnp.float32)
        product = jnp.dot(spin_vals, matrix, preferred_element_type=jnp.float32)
        return 2.0 - jnp.sum(spin_vals * product, axis=1) / weight_total

    blocks = jnp.arange(AMPS // block_len, dtype=jnp.int32)
    return lax.map(one_block, blocks).reshape(AMPS)


def undo_mixer(forward_state, adjoint_state, beta_now, qubit_count):
    cos_beta = jnp.cos(beta_now)
    sin_beta = jnp.sin(beta_now)
    mixing = jnp.zeros((), jnp.float32)
    for qubit_idx in range(qubit_count):
        view_shape = (2, -1, 2, 2 ** qubit_idx)
        psi_view = forward_state.reshape(view_shape)
        lam_view = adjoint_state.reshape(view_shape)
        psi_flip = jnp.flip(psi_view, 2)
        lam_flip = jnp.flip(lam_view, 2)
        mixing = mixing + jnp.sum(lam_view[0] * psi_flip[1] - lam_view[1] * psi_flip[0])
        forward_state = jnp.stack([cos_beta * psi_view[0] - sin_beta * psi_flip[1],
                                   cos_beta * psi_view[1] + sin_beta * psi_flip[0]]).reshape(2, AMPS)
        adjoint_state = jnp.stack([cos_beta * lam_view[0] - sin_beta * lam_flip[1],
                                   cos_beta * lam_view[1] + sin_beta * lam_flip[0]]).reshape(2, AMPS)
    return forward_state, adjoint_state, mixing


def reference(forward, adjoint, edges, weights, layout, slab_bits, angles):
    qubit_count = AMPS.bit_length() - 1
    cost_now = cost_field(edges, weights, layout, slab_bits, qubit_count)
    forward_state = forward
    adjoint_state = adjoint
    gradient_terms = [None] * (2 * LAYERS)
    for layer_idx in reversed(range(LAYERS)):
        gamma_now = angles[2 * layer_idx]
        beta_now = angles[2 * layer_idx + 1]
        forward_state, adjoint_state, mixing = undo_mixer(forward_state, adjoint_state, beta_now, qubit_count)
        gradient_terms[2 * layer_idx + 1] = 2.0 * mixing / AMPS
        intersection = jnp.sum(cost_now * (adjoint_state[0] * forward_state[1] - adjoint_state[1] * forward_state[0]))
        gradient_terms[2 * layer_idx] = 2.0 * intersection / AMPS
        cos_phase = jnp.cos(gamma_now * cost_now)
        sin_phase = jnp.sin(gamma_now * cost_now)
        forward_state = jnp.stack([forward_state[0] * cos_phase - forward_state[1] * sin_phase,
                                   forward_state[1] * cos_phase + forward_state[0] * sin_phase])
        adjoint_state = jnp.stack([adjoint_state[0] * cos_phase - adjoint_state[1] * sin_phase,
                                   adjoint_state[1] * cos_phase + adjoint_state[0] * sin_phase])
    return forward_state, adjoint_state, jnp.stack(gradient_terms)
```

```python
import jax
import jax.numpy as jnp
from jax import lax
from jax.experimental import pallas as pl
from jax.experimental.pallas import tpu as pltpu
from jax.sharding import Mesh, PartitionSpec as P

NODES = 40
LAYERS = 2
LANES = 128
TILE = 8
CORES = 2
F32 = jnp.float32
BF16 = jnp.bfloat16
VMEM_LIMIT = 12 << 20


def vmem_call(body, out_shapes, scratch=(), smem_inputs=(), inputs=(), smem_out=False):
    specs = [pl.BlockSpec(memory_space=pltpu.SMEM)] * len(smem_inputs)
    specs += [pl.BlockSpec(memory_space=pltpu.VMEM)] * len(inputs)
    place = pltpu.SMEM if smem_out else pltpu.VMEM
    return pl.pallas_call(
        body,
        out_shape=[jax.ShapeDtypeStruct(shape, kind) for shape, kind in out_shapes],
        in_specs=specs,
        out_specs=[pl.BlockSpec(memory_space=place)] * len(out_shapes),
        scratch_shapes=list(scratch),
        compiler_params=pltpu.CompilerParams(vmem_limit_bytes=VMEM_LIMIT),
    )(*smem_inputs, *inputs)


def half_angle(x):
    y = 0.5 * x
    z = y * y
    sin_y = jnp.full_like(z, -1.0 / 1307674368000.0)
    for factor in (6227020800.0, -39916800.0, 362880.0, -5040.0, 120.0, -6.0, 1.0):
        sin_y = sin_y * z + 1.0 / factor
    sin_y = sin_y * y
    cos_y = jnp.full_like(z, 1.0 / 20922789888000.0)
    for factor in (-87178291200.0, 479001600.0, -3628800.0, 40320.0, -720.0, 24.0, -2.0, 1.0):
        cos_y = cos_y * z + 1.0 / factor
    return 2.0 * sin_y * cos_y, 1.0 - 2.0 * sin_y * sin_y


def split(value):
    high = value.astype(BF16)
    return high, (value - high.astype(F32)).astype(BF16)


def dot(left, right):
    return jnp.dot(left, right, preferred_element_type=F32)


def mixer_mats(size, cos_beta, sin_beta, least=0):
    row = lax.broadcasted_iota(jnp.int32, (size, size), 0)
    col = lax.broadcasted_iota(jnp.int32, (size, size), 1)
    differ = jnp.bitwise_xor(row, col)
    real = jnp.ones((size, size), F32)
    real = jnp.where(jnp.bitwise_and(differ, (1 << least) - 1) == 0, real, 0.0)
    imag = jnp.zeros((size, size), F32)
    for bit in range(least, size.bit_length() - 1):
        flagged = jnp.bitwise_and(differ, 1 << bit) != 0
        real, imag = (
            jnp.where(flagged, -imag * sin_beta, real * cos_beta),
            jnp.where(flagged, real * sin_beta, imag * cos_beta),
        )
    return real, imag


def flip_mat(size, least=0):
    row = lax.broadcasted_iota(jnp.int32, (size, size), 0)
    col = lax.broadcasted_iota(jnp.int32, (size, size), 1)
    differ = jnp.bitwise_xor(row, col)
    count = jnp.zeros((size, size), jnp.int32)
    for bit in range(size.bit_length() - 1):
        count = count + jnp.bitwise_and(differ >> bit, 1)
    rest = jnp.bitwise_and(differ, (1 << least) - 1)
    return jnp.where(jnp.logical_and(count == 1, rest == 0), 1.0, 0.0).astype(BF16)


def rotate_all(planes, lane_high, lane_low, row_high, row_low, cos_beta, sin_beta):
    low = planes[0].shape[0]
    mixed = []
    for block in planes:
        high, rest = split(block)
        if lane_high is not None:
            lanes = dot(high, lane_high) + dot(rest, lane_high) + dot(high, lane_low)
            high, rest = split(lanes)
        both = dot(row_high, high) + dot(row_high, rest) + dot(row_low, high)
        real = both[:low, :LANES] - both[low:, LANES:]
        imag = both[:low, LANES:] + both[low:, :LANES]
        mixed.append((real, imag))
    stride = 1
    while stride < len(mixed):
        for first in range(len(mixed)):
            if first & stride:
                continue
            (ar, ai), (br, bi) = mixed[first], mixed[first + stride]
            mixed[first] = (cos_beta * ar - sin_beta * bi, cos_beta * ai + sin_beta * br)
            mixed[first + stride] = (cos_beta * br - sin_beta * ai, cos_beta * bi + sin_beta * ar)
        stride *= 2
    return mixed


def flips_all(planes, lane_flip, row_flip):
    out = []
    for index, block in enumerate(planes):
        high, rest = split(block)
        total = dot(row_flip, high) + dot(row_flip, rest)
        if lane_flip is not None:
            total = total + dot(high, lane_flip) + dot(rest, lane_flip)
        stride = 1
        while stride < len(planes):
            total = total + planes[index ^ stride]
            stride *= 2
        out.append(total)
    return out


def fold_rows(value):
    folded = value[:TILE]
    for start in range(TILE, value.shape[0], TILE):
        folded = folded + value[start : start + TILE]
    return jnp.sum(folded, axis=0, keepdims=True)


def cross_imag(lam, other):
    return fold_rows(lam[:, :LANES] * other[:, LANES:] - lam[:, LANES:] * other[:, :LANES])


def spin_rows(position, layout, slab, known):
    lane_bits = LANES.bit_length() - 1
    shift = jnp.clip(layout - lane_bits, 0, known - 1)
    inside = jnp.bitwise_and(jnp.right_shift(position, shift), 1)
    bit = jnp.where(layout < known + lane_bits, inside, slab)
    return jnp.where(layout < lane_bits, 0, 1 - 2 * bit).astype(F32)


def table_body(row_count, place_first, place_second, known, low):
    lane_bits = LANES.bit_length() - 1

    def body(angles, edges, weights, layout, slab, *outs):
        cost_a, cos_a, sin_a, cost_b, cos_b, sin_b = outs[:6]
        mats = outs[6:]
        node = lax.broadcasted_iota(jnp.int32, (edges.shape[0], NODES), 1)
        first = jnp.where(edges[:, 0:1] == node, 1.0, 0.0)
        second = jnp.where(edges[:, 1:2] == node, 1.0, 0.0)
        weight = weights[...].astype(F32)
        total = jnp.sum(weight, axis=0, keepdims=True)
        across = (((0,), (0,)), ((), ()))
        exact = lax.Precision.HIGHEST

        def full(left, right, dims):
            return lax.dot_general(left, right, dims, precision=exact, preferred_element_type=F32)

        matrix = full(first * weight, second, across) + full(second * weight, first, across)
        lane = lax.broadcasted_iota(jnp.int32, (LANES, NODES), 0)
        lane_layout = layout[...]
        lane_bit = jnp.bitwise_and(jnp.right_shift(lane, jnp.clip(lane_layout, 0, lane_bits - 1)), 1)
        lane_spin = jnp.where(lane_layout < lane_bits, 1 - 2 * lane_bit, 0).astype(F32)
        plain = (((1,), (0,)), ((), ()))
        turned = (((1,), (1,)), ((), ()))
        lane_energy = full(jnp.ones((TILE, NODES), F32), lane_spin * full(lane_spin, matrix, plain), turned)[0:1]

        def field(position, cost, cos_out, sin_out, gamma):
            spins = spin_rows(position, lane_layout, slab[...], known)
            pulled = full(spins, matrix, plain)
            energy = jnp.sum(pulled * spins, axis=1, keepdims=True)
            energy = energy + lane_energy + 2.0 * full(pulled, lane_spin, turned)
            value = 2.0 - energy / total
            cost[...] = value
            sine, cosine = half_angle(gamma * value)
            cos_out[...] = cosine
            sin_out[...] = sine

        row = lax.broadcasted_iota(jnp.int32, (row_count, 1), 0)
        field(place_first(row), cost_a, cos_a, sin_a, angles[0])
        field(place_second(row), cost_b, cos_b, sin_b, angles[2])
        for layer in range(LAYERS):
            sine, cosine = half_angle(jnp.full((1, 1), angles[2 * layer + 1], F32))
            real, imag = mixer_mats(LANES, cosine, sine)
            lanes = jnp.concatenate(
                [jnp.concatenate([real, imag], axis=1), jnp.concatenate([-imag, real], axis=1)], axis=0
            )
            mats[4 * layer][...], mats[4 * layer + 1][...] = split(lanes)
            real, imag = mixer_mats(low, cosine, sine)
            mats[4 * layer + 2][...], mats[4 * layer + 3][...] = split(jnp.concatenate([real, imag], axis=0))

    return body


def make_tables(angles, edges, weights, layout, slab, rows, low, place_first, place_second, known):
    grid = ((rows, LANES), F32)
    shapes = [grid] * 6
    for _ in range(LAYERS):
        shapes += [((2 * LANES, 2 * LANES), BF16)] * 2 + [((2 * low, low), BF16)] * 2
    out = vmem_call(
        table_body(rows, place_first, place_second, known, low),
        shapes,
        smem_inputs=(angles,),
        inputs=(edges, weights, layout, slab),
    )
    return out[:3], out[3:6], [out[6 + 4 * layer : 10 + 4 * layer] for layer in range(LAYERS)]


class Shape:
    def __init__(self, groups, depth, amp_dev):
        self.groups = groups
        self.depth = depth
        self.wide = groups * CORES
        self.devices = self.wide * depth
        self.rows = amp_dev // LANES
        self.part = self.rows // self.devices
        self.low = min(self.rows, 2 * LANES)
        self.known = (self.rows * self.devices).bit_length() - 1
        self.planes = self.rows // self.low

    def piece(self, wide, level):
        return ((wide // CORES) * self.depth + level) * CORES + wide % CORES


def slots(shape):
    return [(k, w) for k in range(shape.depth) for w in range(shape.wide)]


def angle_pair(angle):
    return half_angle(jnp.full((TILE, LANES), angle, F32))


def butterflies(real, imag, tangent, scale):
    count = len(real)
    stride = 1
    while stride < count:
        for first in range(count):
            if first & stride:
                continue
            other = first + stride
            ar, ai, br, bi = real[first], imag[first], real[other], imag[other]
            real[first], imag[first] = ar - tangent * bi, ai + tangent * br
            real[other], imag[other] = br - tangent * ai, bi + tangent * ar
        stride *= 2
    return [scale * v for v in real], [scale * v for v in imag]


def flip_sum(values, index):
    total = None
    stride = 1
    while stride < len(values):
        term = values[index ^ stride]
        total = term if total is None else total + term
        stride *= 2
    return total


def mixer_scale(sine, cosine, count):
    scale = cosine
    for _ in range(count - 1):
        scale = scale * cosine
    return sine / cosine, scale


def load_pair(ref, piece, part, start):
    base = (piece * part + start) * 2
    return (
        ref[pl.ds(base, TILE, stride=2), :],
        ref[pl.ds(base + 1, TILE, stride=2), :],
    )


def ordered_slots(shape):
    return slots(shape)


def level_now(shape):
    return lax.axis_index("z")


def pre_body(shape, by_level):
    part = shape.part

    def body(angles, state, *outs):
        level = level_now(shape)
        sine, cosine = angle_pair(angles[3])
        order = ordered_slots(shape)
        tangent, scale = mixer_scale(sine, cosine, shape.devices.bit_length() - 1)
        for start in range(0, part, TILE):
            real, imag = [], []
            for k, w in order:
                piece = shape.piece(w, jnp.bitwise_xor(level, k))
                re, im = load_pair(state, piece, part, start)
                real.append(re)
                imag.append(im)
            real, imag = butterflies(real, imag, tangent, scale)
            for (k, w), re, im in zip(order, real, imag):
                if by_level:
                    ref, base = outs[k], w * 2 * part + start
                else:
                    ref, base = outs[0], (w * shape.depth + k) * 2 * part + start
                ref[base : base + TILE, :] = re
                ref[base + part : base + part + TILE, :] = im

    return body


def level_shape(shape):
    return ((shape.wide * 2 * shape.part, LANES), F32)


def whole_shape(shape):
    return ((shape.devices * 2 * shape.part, LANES), F32)


def pre(shape, angles, state, by_level):
    outs = [level_shape(shape)] * shape.depth if by_level else [whole_shape(shape)]
    return vmem_call(pre_body(shape, by_level), outs, smem_inputs=(angles,), inputs=(state,))


def flip_pre(shape, forward, adjoint):
    part = shape.part

    def body(psi, lam, out):
        total = None
        for start in range(0, part, TILE):
            real, imag = [], []
            for piece in range(shape.devices):
                re, im = load_pair(psi, piece, part, start)
                real.append(re)
                imag.append(im)
            for piece in range(shape.devices):
                re, im = load_pair(lam, piece, part, start)
                term = re * flip_sum(imag, piece) - im * flip_sum(real, piece)
                total = term if total is None else total + term
        out[...] = jnp.sum(total, axis=0, keepdims=True)

    return vmem_call(body, [((1, LANES), F32)], inputs=(forward, adjoint))[0]


def swap_order(shape, arrays, join):
    size = 2 * shape.part

    def body(*refs):
        for k in range(shape.depth):
            for w in range(shape.wide):
                base = (w * shape.depth + k) * size
                if join:
                    refs[-1][base : base + size, :] = refs[k][w * size : (w + 1) * size, :]
                else:
                    refs[1 + k][w * size : (w + 1) * size, :] = refs[0][base : base + size, :]

    outs = [whole_shape(shape)] if join else [level_shape(shape)] * shape.depth
    out = vmem_call(body, outs, inputs=tuple(arrays))
    return out[0] if join else out


def slot_place(shape, refs, k, w):
    if len(refs) == 1:
        return refs[0], (w * shape.depth + k) * 2 * shape.part
    return refs[k], w * 2 * shape.part


def load_planes(shape, refs):
    part = shape.part
    pairs = []
    for k, w in slots(shape):
        ref, base = slot_place(shape, refs, k, w)
        pairs.append(jnp.concatenate([ref[base : base + part, :], ref[base + part : base + 2 * part, :]], axis=1))
    per = shape.low // part
    return [jnp.concatenate(pairs[i * per : (i + 1) * per], axis=0) for i in range(shape.planes)]


def phased(real, imag, cosine, sine):
    return real * cosine - imag * sine, imag * cosine + real * sine


def mid_math(shape, angles, planes, mats, cos_b, sin_b):
    low = shape.low
    sine, cosine = half_angle(jnp.full((1, 1), angles[3], F32))
    first = rotate_all(planes, *[m[...] for m in mats[4:8]], cosine, sine)
    turned = []
    for i, (re, im) in enumerate(first):
        re, im = phased(re, im, cos_b[i * low : (i + 1) * low, :], sin_b[i * low : (i + 1) * low, :])
        turned.append(jnp.concatenate([re, im], axis=1))
    sine, cosine = half_angle(jnp.full((1, 1), angles[1], F32))
    second = rotate_all(turned, *[m[...] for m in mats[0:4]], cosine, sine)
    return first, second


def mid(shape, angles, arrays, field_b, mats, by_level):
    count = len(arrays)
    part = shape.part

    def body(*refs):
        angle = refs[0]
        states = refs[1 : 1 + count]
        cos_b, sin_b = refs[1 + count : 3 + count]
        matrices = refs[3 + count : 11 + count]
        before = refs[11 + count]
        outs = refs[12 + count :]
        first, second = mid_math(shape, angle, load_planes(shape, states), matrices, cos_b, sin_b)
        for i, (re, im) in enumerate(first):
            before[i * shape.low : (i + 1) * shape.low, :LANES] = re
            before[i * shape.low : (i + 1) * shape.low, LANES:] = im
        per = shape.low // part
        for i, (k, w) in enumerate(slots(shape)):
            re, im = second[i // per]
            at = (i % per) * part
            ref, base = slot_place(shape, outs, k, w)
            ref[base : base + part, :] = re[at : at + part]
            ref[base + part : base + 2 * part, :] = im[at : at + part]

    outs = [((shape.rows, 2 * LANES), F32)]
    outs += [level_shape(shape)] * shape.depth if by_level else [whole_shape(shape)]
    result = vmem_call(
        body,
        outs,
        smem_inputs=(angles,),
        inputs=tuple(arrays) + (field_b[1], field_b[2]) + tuple(mats[0]) + tuple(mats[1]),
    )
    return result[0], result[1:]


def gradients_mid(shape, cost_b, psi_before, lam_before, psi_after, lam_after, canonical=False):
    n_psi, n_lam = len(psi_after), len(lam_after)
    low = shape.low

    def body(*refs):
        cost, psi_ref, lam_ref = refs[:3]
        psi_refs = refs[3 : 3 + n_psi]
        lam_refs = refs[3 + n_psi : 3 + n_psi + n_lam]
        out = refs[-1]
        small = flip_mat(LANES)
        zero = jnp.zeros_like(small)
        lane_flip = jnp.concatenate(
            [jnp.concatenate([small, zero], axis=1), jnp.concatenate([zero, small], axis=1)], axis=0
        )
        row_flip = flip_mat(low)
        spans = [slice(i * low, (i + 1) * low) for i in range(shape.planes)]
        psi = [psi_ref[span, :] for span in spans]
        lam = [lam_ref[span, :] for span in spans]
        inter = jnp.zeros((1, LANES), F32)
        mix_one = jnp.zeros((1, LANES), F32)
        for i, flips in enumerate(flips_all(psi, lane_flip, row_flip)):
            mix_one = mix_one + cross_imag(lam[i], flips)
            weighted = jnp.concatenate([cost[spans[i], :]] * 2, axis=1) * psi[i]
            inter = inter + cross_imag(lam[i], weighted)
        if canonical:
            psi = [psi_refs[0][span, :] for span in spans]
            lam = [lam_refs[0][span, :] for span in spans]
        else:
            psi = load_planes(shape, psi_refs)
            lam = load_planes(shape, lam_refs)
        mix_zero = jnp.zeros((1, LANES), F32)
        for i, flips in enumerate(flips_all(psi, lane_flip, row_flip)):
            mix_zero = mix_zero + cross_imag(lam[i], flips)
        out[...] = jnp.concatenate([mix_zero, inter, mix_one], axis=0)

    return vmem_call(
        body,
        [((3, LANES), F32)],
        inputs=(cost_b, psi_before, lam_before) + tuple(psi_after) + tuple(lam_after),
    )[0]


def load_slots(shape, refs, start):
    part = shape.part
    real, imag = [], []
    for k, w in ordered_slots(shape):
        ref, base = slot_place(shape, refs, k, w)
        real.append(ref[base + start : base + start + TILE, :])
        imag.append(ref[base + part + start : base + part + start + TILE, :])
    return real, imag


def post_mix(shape, angles, arrays):
    count = len(arrays)
    part = shape.part
    half = shape.devices * part

    def body(*refs):
        angle, states = refs[0], refs[1 : 1 + count]
        mixed, flipped = refs[1 + count :]
        sine, cosine = angle_pair(angle[1])
        tangent, scale = mixer_scale(sine, cosine, shape.devices.bit_length() - 1)
        for start in range(0, part, TILE):
            real, imag = load_slots(shape, states, start)
            real, imag = butterflies(real, imag, tangent, scale)
            for i in range(shape.devices):
                base = i * part + start
                mixed[base : base + TILE, :] = real[i]
                mixed[half + base : half + base + TILE, :] = imag[i]
                flipped[base : base + TILE, :] = flip_sum(real, i)
                flipped[half + base : half + base + TILE, :] = flip_sum(imag, i)

    shapes = [((2 * half, LANES), F32)] * 2
    return vmem_call(body, shapes, smem_inputs=(angles,), inputs=tuple(arrays))


def post_mix_grads(shape, angles, arrays, mixed_psi, flips_psi, cost_a):
    count = len(arrays)
    part = shape.part
    half = shape.devices * part

    def body(*refs):
        angle, states = refs[0], refs[1 : 1 + count]
        psi, flips, cost = refs[1 + count : 4 + count]
        mixed, out = refs[4 + count :]
        level = level_now(shape)
        order = ordered_slots(shape)
        sine, cosine = angle_pair(angle[1])
        tangent, scale = mixer_scale(sine, cosine, shape.devices.bit_length() - 1)
        mix = jnp.zeros((TILE, LANES), F32)
        inter = jnp.zeros((TILE, LANES), F32)
        for start in range(0, part, TILE):
            real, imag = load_slots(shape, states, start)
            real, imag = butterflies(real, imag, tangent, scale)
            for i, (k, w) in enumerate(order):
                base = i * part + start
                high = half + base
                mixed[base : base + TILE, :] = real[i]
                mixed[high : high + TILE, :] = imag[i]
                mix = mix + real[i] * flips[high : high + TILE, :] - imag[i] * flips[base : base + TILE, :]
                piece = shape.piece(w, jnp.bitwise_xor(level, k))
                value = cost[pl.ds(pl.multiple_of(piece * part + start, TILE), TILE), :]
                inter = inter + value * (
                    real[i] * psi[high : high + TILE, :] - imag[i] * psi[base : base + TILE, :]
                )
        out[0:1, :] = jnp.sum(inter, axis=0, keepdims=True)
        out[1:2, :] = jnp.sum(mix, axis=0, keepdims=True)

    shapes = [((2 * half, LANES), F32), ((2, LANES), F32)]
    return vmem_call(
        body, shapes, smem_inputs=(angles,), inputs=tuple(arrays) + (mixed_psi, flips_psi, cost_a)
    )


def post_phase(shape, mixed, field_a):
    part = shape.part
    half = shape.devices * part

    def body(state, cos_a, sin_a, out):
        level = level_now(shape)
        for i, (k, w) in enumerate(ordered_slots(shape)):
            piece = shape.piece(w, jnp.bitwise_xor(level, k))
            for start in range(0, part, TILE):
                base = i * part + start
                real = state[base : base + TILE, :]
                imag = state[half + base : half + base + TILE, :]
                row = pl.multiple_of(piece * part + start, TILE)
                re, im = phased(real, imag, cos_a[pl.ds(row, TILE), :], sin_a[pl.ds(row, TILE), :])
                out[pl.ds(2 * row, TILE, stride=2), :] = re
                out[pl.ds(2 * row + 1, TILE, stride=2), :] = im

    return vmem_call(body, [((2 * half, LANES), F32)], inputs=(mixed, field_a[1], field_a[2]))[0]


def send_levels(shape, arrays):
    out = [arrays[0]]
    for k in range(1, shape.depth):
        pairs = [(i, i ^ k) for i in range(shape.depth)]
        out.append(lax.ppermute(arrays[k], "z", pairs))
    return out


def send_wide(shape, array):
    block = array.reshape(shape.wide, -1, LANES)
    return lax.all_to_all(block, ("grp", "core"), 0, 0, tiled=True).reshape(array.shape)


def total_grads(shape, parts):
    count = shape.devices

    def join(*refs):
        early, mid_part, late, out = refs
        rows = [late[0:1, :], late[1:2, :] + mid_part[0:1, :], mid_part[1:2, :], mid_part[2:3, :] + early[...]]
        block = jnp.concatenate(rows + [jnp.zeros((TILE - 4, LANES), F32)], axis=0)
        for i in range(count):
            out[i * TILE : (i + 1) * TILE, :] = block

    block = vmem_call(join, [((count * TILE, LANES), F32)], inputs=tuple(parts))[0]
    every = lax.all_to_all(
        block.reshape(count, TILE, LANES), ("grp", "z", "core"), 0, 0, tiled=True
    ).reshape(count * TILE, LANES)
    scale = 2.0 / (shape.rows * LANES * count)

    def finish(refs, out):
        block = refs[0:TILE, :]
        for i in range(1, count):
            block = block + refs[i * TILE : (i + 1) * TILE, :]
        block = jnp.sum(block, axis=1, keepdims=True) * scale
        for i in range(2 * LAYERS):
            out[i] = jnp.sum(block[i : i + 1, :])

    return vmem_call(finish, [((2 * LAYERS,), F32)], inputs=(every,), smem_out=True)[0]


def after(values, first):
    return lax.optimization_barrier((values, first))[0]


def piece_mix(shape, angles, which, state):
    low = shape.low
    least = shape.part.bit_length() - 1

    def body(angle, ref, mixed, flipped):
        sine, cosine = half_angle(jnp.full((1, 1), angle[which], F32))
        real, imag = mixer_mats(low, cosine, sine, least)
        row_high, row_low = split(jnp.concatenate([real, imag], axis=0))
        row_flip = flip_mat(low, least)
        blocks = [ref[i * low : (i + 1) * low, :] for i in range(shape.planes)]
        for i, (re, im) in enumerate(rotate_all(blocks, None, None, row_high, row_low, cosine, sine)):
            mixed[i * low : (i + 1) * low, :LANES] = re
            mixed[i * low : (i + 1) * low, LANES:] = im
        for i, block in enumerate(flips_all(blocks, None, row_flip)):
            flipped[i * low : (i + 1) * low, :] = block

    return vmem_call(
        body, [((shape.rows, 2 * LANES), F32)] * 2, smem_inputs=(angles,), inputs=(state,)
    )


def plain_cross(lam, other):
    def body(lam_ref, other_ref, out):
        out[...] = cross_imag(lam_ref[...], other_ref[...])

    return vmem_call(body, [((1, LANES), F32)], inputs=(lam, other))[0]


def plain_phase(shape, state, field, gradient):
    def body(ref, cost, cosine, sine, out):
        real, imag = ref[:, :LANES], ref[:, LANES:]
        if gradient:
            re, im = cost[...] * real, cost[...] * imag
        else:
            re, im = phased(real, imag, cosine[...], sine[...])
        out[:, :LANES] = re
        out[:, LANES:] = im

    return vmem_call(body, [((shape.rows, 2 * LANES), F32)], inputs=(state,) + tuple(field))[0]


def plain_mid(shape, angles, state, field_b, mats):
    low = shape.low

    def body(angle, ref, cos_b, sin_b, *rest):
        blocks = [ref[i * low : (i + 1) * low, :] for i in range(shape.planes)]
        for out, pairs in zip(rest[8:], mid_math(shape, angle, blocks, rest[:8], cos_b, sin_b)):
            for i, (re, im) in enumerate(pairs):
                out[i * low : (i + 1) * low, :LANES] = re
                out[i * low : (i + 1) * low, LANES:] = im

    return vmem_call(
        body,
        [((shape.rows, 2 * LANES), F32)] * 2,
        smem_inputs=(angles,),
        inputs=(state, field_b[1], field_b[2]) + tuple(mats[0]) + tuple(mats[1]),
    )


def exchange_all(shape, state):
    block = state.reshape(shape.devices, -1, 2 * LANES)
    return lax.all_to_all(block, ("grp", "z", "core"), 0, 0, tiled=True).reshape(state.shape)


def plain(shape, forward, adjoint, edges, weights, layout, slab_bits, angles):
    rows = shape.rows

    def wide(array):
        return array.reshape(2, rows, LANES).transpose(1, 0, 2).reshape(rows, 2 * LANES)

    def narrow(array):
        return array.reshape(rows, 2, LANES).transpose(1, 0, 2).reshape(2, rows * LANES)

    def device():
        return shape.piece(lax.axis_index("grp") * CORES + lax.axis_index("core"), lax.axis_index("z"))

    def before(row):
        return device() * rows + row

    def beyond(row):
        return (row // shape.part) * rows + device() * shape.part + row % shape.part

    small = (angles, edges, weights.reshape(-1, 1), layout.reshape(1, -1), slab_bits.reshape(1, -1))
    field_a, field_b, mats = make_tables(*small, rows, shape.low, before, beyond, shape.known)
    psi, flips = piece_mix(shape, angles, 3, wide(forward))
    lam, _ = piece_mix(shape, angles, 3, wide(adjoint))
    early = plain_cross(wide(adjoint), flips)
    psi_before, psi_after = plain_mid(shape, angles, exchange_all(shape, psi), field_b, mats)
    lam_before, lam_after = plain_mid(shape, angles, exchange_all(shape, lam), field_b, mats)
    mid_part = gradients_mid(shape, field_b[0], psi_before, lam_before, [psi_after], [lam_after], True)
    psi, lam = exchange_all(shape, psi_after), exchange_all(shape, lam_after)
    psi_mixed, flips = piece_mix(shape, angles, 1, psi)
    lam_mixed, _ = piece_mix(shape, angles, 1, lam)
    late = jnp.concatenate(
        [plain_cross(lam_mixed, plain_phase(shape, psi_mixed, field_a, True)), plain_cross(lam, flips)], axis=0
    )
    grads = total_grads(shape, (early, mid_part, late))
    outs = [narrow(plain_phase(shape, state, field_a, False)) for state in (psi_mixed, lam_mixed)]
    return outs[0], outs[1], grads


def interleave(array, rows):
    return array.reshape(2, rows, LANES).transpose(1, 0, 2).reshape(2 * rows, LANES)


def deinterleave(array, rows):
    return array.reshape(rows, 2, LANES).transpose(1, 0, 2).reshape(2, rows * LANES)


def places(shape):
    def device():
        return shape.piece(lax.axis_index("grp") * CORES + lax.axis_index("core"), lax.axis_index("z"))

    def before(row):
        return device() * shape.rows + row

    def beyond(row):
        slot, inner = row // shape.part, row % shape.part
        source = shape.piece(slot % shape.wide, jnp.bitwise_xor(slot // shape.wide, lax.axis_index("z")))
        return source * shape.rows + device() * shape.part + inner

    return before, beyond


def pipelined(shape, forward, adjoint, edges, weights, layout, slab_bits, angles):
    rows = shape.rows
    psi_raw, lam_raw = interleave(forward, rows), interleave(adjoint, rows)
    psi = pre(shape, angles, psi_raw, True)
    psi = send_levels(shape, psi)
    lam = pre(shape, angles, lam_raw, False)
    lam = send_wide(shape, lam[0])
    before, beyond = places(shape)
    small = after((angles, edges, weights.reshape(-1, 1), layout.reshape(1, -1), slab_bits.reshape(1, -1)), psi[0])
    field_a, field_b, mats = make_tables(*small, rows, shape.low, before, beyond, shape.known)
    early = flip_pre(shape, psi_raw, lam_raw)
    lam = swap_order(shape, [lam], False)
    lam = send_levels(shape, lam)
    psi = send_wide(shape, swap_order(shape, psi, True))
    psi_before, psi = mid(shape, angles, [psi], field_b, mats, True)
    psi_after = psi
    psi = send_levels(shape, psi)
    lam_before, lam = mid(shape, angles, lam, field_b, mats, False)
    lam_after = lam
    lam = send_wide(shape, lam[0])
    mid_part = gradients_mid(shape, field_b[0], psi_before, lam_before, psi_after, lam_after)
    lam = swap_order(shape, [lam], False)
    lam = send_levels(shape, lam)
    psi = send_wide(shape, swap_order(shape, psi, True))
    psi_mixed, psi_flips = post_mix(shape, angles, [psi])
    lam_mixed, late = post_mix_grads(shape, angles, lam, psi_mixed, psi_flips, field_a[0])
    grads = total_grads(shape, (early, mid_part, late))
    psi_out = post_phase(shape, psi_mixed, field_a)
    lam_out = post_phase(shape, lam_mixed, field_a)
    return deinterleave(psi_out, rows), deinterleave(lam_out, rows), grads


def solution(mesh):
    groups, rest = mesh.shape["grp"], mesh.shape["rep"]
    depth = rest // CORES
    fine = Mesh(mesh.devices.reshape(groups, depth, CORES), ("grp", "z", "core"))

    def per_device(forward, *others):
        shape = Shape(groups, depth, forward.shape[1])
        whole_tiles = shape.part % TILE == 0
        return (pipelined if whole_tiles else plain)(shape, forward, *others)

    state = P(None, ("grp", "z", "core"))
    return jax.shard_map(
        per_device,
        mesh=fine,
        in_specs=(state, state, P(), P(), P(), P(), P()),
        out_specs=(state, state, P()),
        check_vma=False,
    )
```

```python
import jax
import jax.numpy as jnp
from jax import lax
from jax.experimental import pallas as pl
from jax.experimental.pallas import tpu as pltpu
from jax.sharding import Mesh, PartitionSpec as P

NODES = 40
LAYERS = 2
LANES = 128
TILE = 8
CORES = 2
F32 = jnp.float32
BF16 = jnp.bfloat16
VMEM_LIMIT = 12 << 20
VMEM_FIRST = 62 << 20


def vmem_call(name, body, out_shapes, inputs=(), smem_out=False, hold=()):
    if hold:
        taken = len(inputs)
        inner = body

        def body(*refs):
            inner(*refs[:taken], *refs[taken + len(hold) :])

        inputs = tuple(inputs) + tuple(hold)
    specs = [pl.BlockSpec(memory_space=pltpu.VMEM)] * len(inputs)
    place = pltpu.SMEM if smem_out else pltpu.VMEM
    return pl.pallas_call(
        body,
        name=name,
        out_shape=[jax.ShapeDtypeStruct(shape, kind) for shape, kind in out_shapes],
        in_specs=specs,
        out_specs=[pl.BlockSpec(memory_space=place)] * len(out_shapes),
        compiler_params=pltpu.CompilerParams(vmem_limit_bytes=VMEM_LIMIT),
    )(*inputs)


def half_angle(x):
    y = 0.5 * x
    z = y * y
    sin_y = jnp.full_like(z, -1.0 / 1307674368000.0)
    for factor in (6227020800.0, -39916800.0, 362880.0, -5040.0, 120.0, -6.0, 1.0):
        sin_y = sin_y * z + 1.0 / factor
    sin_y = sin_y * y
    cos_y = jnp.full_like(z, 1.0 / 20922789888000.0)
    for factor in (-87178291200.0, 479001600.0, -3628800.0, 40320.0, -720.0, 24.0, -2.0, 1.0):
        cos_y = cos_y * z + 1.0 / factor
    return 2.0 * sin_y * cos_y, 1.0 - 2.0 * sin_y * sin_y


def split(value):
    high = value.astype(BF16)
    return high, (value - high.astype(F32)).astype(BF16)


def dot(left, right):
    return jnp.dot(left, right, preferred_element_type=F32)


def mixer_mats(size, cos_beta, sin_beta, least=0):
    row = lax.broadcasted_iota(jnp.int32, (size, size), 0)
    col = lax.broadcasted_iota(jnp.int32, (size, size), 1)
    differ = jnp.bitwise_xor(row, col)
    real = jnp.ones((size, size), F32)
    real = jnp.where(jnp.bitwise_and(differ, (1 << least) - 1) == 0, real, 0.0)
    imag = jnp.zeros((size, size), F32)
    for bit in range(least, size.bit_length() - 1):
        flagged = jnp.bitwise_and(differ, 1 << bit) != 0
        real, imag = (
            jnp.where(flagged, -imag * sin_beta, real * cos_beta),
            jnp.where(flagged, real * sin_beta, imag * cos_beta),
        )
    return real, imag


def flip_mat(size, least=0):
    row = lax.broadcasted_iota(jnp.int32, (size, size), 0)
    col = lax.broadcasted_iota(jnp.int32, (size, size), 1)
    differ = jnp.bitwise_xor(row, col)
    count = jnp.zeros((size, size), jnp.int32)
    for bit in range(size.bit_length() - 1):
        count = count + jnp.bitwise_and(differ >> bit, 1)
    rest = jnp.bitwise_and(differ, (1 << least) - 1)
    return jnp.where(jnp.logical_and(count == 1, rest == 0), 1.0, 0.0).astype(BF16)


def rotate_all(planes, lane_high, lane_low, row_high, row_low, cos_beta, sin_beta):
    low = planes[0].shape[0]
    mixed = []
    for block in planes:
        high, rest = split(block)
        if lane_high is not None:
            lanes = dot(high, lane_high) + dot(rest, lane_high) + dot(high, lane_low)
            high, rest = split(lanes)
        both = dot(row_high, high) + dot(row_high, rest) + dot(row_low, high)
        real = both[:low, :LANES] - both[low:, LANES:]
        imag = both[:low, LANES:] + both[low:, :LANES]
        mixed.append((real, imag))
    stride = 1
    while stride < len(mixed):
        for first in range(len(mixed)):
            if first & stride:
                continue
            (ar, ai), (br, bi) = mixed[first], mixed[first + stride]
            mixed[first] = (cos_beta * ar - sin_beta * bi, cos_beta * ai + sin_beta * br)
            mixed[first + stride] = (cos_beta * br - sin_beta * ai, cos_beta * bi + sin_beta * ar)
        stride *= 2
    return mixed


def flips_all(planes, lane_flip, row_flip):
    out = []
    for index, block in enumerate(planes):
        high, rest = split(block)
        total = dot(row_flip, high) + dot(row_flip, rest)
        if lane_flip is not None:
            total = total + dot(high, lane_flip) + dot(rest, lane_flip)
        stride = 1
        while stride < len(planes):
            total = total + planes[index ^ stride]
            stride *= 2
        out.append(total)
    return out


def fold_rows(value):
    folded = value[:TILE]
    for start in range(TILE, value.shape[0], TILE):
        folded = folded + value[start : start + TILE]
    return jnp.sum(folded, axis=0, keepdims=True)


def cross_imag(lam, other):
    return fold_rows(lam[:, :LANES] * other[:, LANES:] - lam[:, LANES:] * other[:, :LANES])


def spin_rows(position, layout, slab, known):
    lane_bits = LANES.bit_length() - 1
    shift = jnp.clip(layout - lane_bits, 0, known - 1)
    inside = jnp.bitwise_and(jnp.right_shift(position, shift), 1)
    bit = jnp.where(layout < known + lane_bits, inside, slab)
    return jnp.where(layout < lane_bits, 0, 1 - 2 * bit).astype(F32)


def field_body(place_first, place_second, known):
    lane_bits = LANES.bit_length() - 1

    def body(angles, edges, weights, layout, slab, cost_a, cos_a, sin_a, cost_b, cos_b, sin_b):
        node = lax.broadcasted_iota(jnp.int32, (NODES, edges.shape[1]), 0)
        first = jnp.where(edges[0:1, :] == node, 1.0, 0.0)
        second = jnp.where(edges[1:2, :] == node, 1.0, 0.0)
        weight = weights[...].astype(F32)
        total = jnp.sum(weight, axis=1, keepdims=True)
        exact = lax.Precision.HIGHEST

        def full(left, right, dims):
            return lax.dot_general(left, right, dims, precision=exact, preferred_element_type=F32)

        plain = (((1,), (0,)), ((), ()))
        turned = (((1,), (1,)), ((), ()))
        matrix = full(first * weight, second, turned) + full(second * weight, first, turned)
        lane = lax.broadcasted_iota(jnp.int32, (LANES, NODES), 0)
        lane_layout = layout[...]
        lane_bit = jnp.bitwise_and(jnp.right_shift(lane, jnp.clip(lane_layout, 0, lane_bits - 1)), 1)
        lane_spin = jnp.where(lane_layout < lane_bits, 1 - 2 * lane_bit, 0).astype(F32)
        lane_energy = full(jnp.ones((TILE, NODES), F32), lane_spin * full(lane_spin, matrix, plain), turned)[0:1]

        def field(position, cost, cos_out, sin_out, gamma):
            spins = spin_rows(position, lane_layout, slab[...], known)
            pulled = full(spins, matrix, plain)
            energy = jnp.sum(pulled * spins, axis=1, keepdims=True)
            energy = energy + lane_energy + 2.0 * full(pulled, lane_spin, turned)
            value = 2.0 - energy / total
            cost[...] = value
            sine, cosine = half_angle(gamma * value)
            cos_out[...] = cosine
            sin_out[...] = sine

        row = lax.broadcasted_iota(jnp.int32, (cost_a.shape[0], 1), 0)
        field(place_first(row), cost_a, cos_a, sin_a, angles[0:1, 0:1])
        row = lax.broadcasted_iota(jnp.int32, (cost_b.shape[0], 1), 0)
        field(place_second(row), cost_b, cos_b, sin_b, angles[0:1, 2:3])
    return body


def make_fields(angles, edges, weights, layout, slab, rows, place_first, place_second, known, core=None, hold=()):
    inner = field_body(place_first, place_second, known)
    shapes = [((rows[0], LANES), F32)] * 3 + [((rows[1], LANES), F32)] * 3
    small = (angles, edges, weights, layout, slab)
    held = tuple(hold)

    def body(*refs):
        refs = refs[: len(small)] + refs[len(small) + len(held) :]
        if core is None:
            inner(*refs)
        else:

            @pl.when(lax.axis_index("core") == core)
            def _():
                inner(*refs)

    return pl.pallas_call(
        body,
        name="make_fields",
        out_shape=[jax.ShapeDtypeStruct(size, kind) for size, kind in shapes],
        in_specs=[pl.BlockSpec(memory_space=pltpu.VMEM)] * (len(small) + len(held)),
        out_specs=[pl.BlockSpec(memory_space=pltpu.VMEM)] * len(shapes),
        input_output_aliases={len(small) + i: i for i in range(len(shapes))} if len(held) == len(shapes) else {},
        compiler_params=pltpu.CompilerParams(vmem_limit_bytes=VMEM_LIMIT),
    )(*small, *held)


def make_mats(angles, low, hold=()):
    def body(angles, *mats):
        for layer in range(LAYERS):
            sine, cosine = half_angle(angles[0:1, 2 * layer + 1 : 2 * layer + 2])
            real, imag = mixer_mats(LANES, cosine, sine)
            lanes = jnp.concatenate(
                [jnp.concatenate([real, imag], axis=1), jnp.concatenate([-imag, real], axis=1)], axis=0
            )
            mats[4 * layer][...], mats[4 * layer + 1][...] = split(lanes)
            real, imag = mixer_mats(low, cosine, sine)
            mats[4 * layer + 2][...], mats[4 * layer + 3][...] = split(jnp.concatenate([real, imag], axis=0))

    shapes = ([((2 * LANES, 2 * LANES), BF16)] * 2 + [((2 * low, low), BF16)] * 2) * LAYERS
    out = vmem_call("make_mats", body, shapes, inputs=(angles,), hold=hold)
    return [out[4 * layer : 4 + 4 * layer] for layer in range(LAYERS)]


def small_inputs(edges, weights, layout, slab_bits):
    return edges.T, weights.reshape(1, -1), layout.reshape(1, -1), slab_bits.reshape(1, -1)


class Shape:
    def __init__(self, groups, depth, amp_dev):
        self.groups = groups
        self.depth = depth
        self.devices = groups * depth * CORES
        self.rows = amp_dev // LANES
        self.known = (self.rows * self.devices).bit_length() - 1
        self.tiles = groups == depth and self.rows % (groups * depth * TILE) == 0
        self.part = self.rows // (groups * depth if self.tiles else self.devices)
        self.low = depth * self.part if self.tiles else min(self.rows, 2 * LANES)
        self.planes = self.rows // self.low

    def own(self):
        return self.chip() * CORES + lax.axis_index("core")

    def chip(self):
        return lax.axis_index("grp") * self.depth + lax.axis_index("z")

    def slots(self):
        return [(u, v) for u in range(self.depth) for v in range(self.depth)]

    def bits(self, letters):
        each = self.depth.bit_length() - 1
        return [bit + (each if letter == "u" else 0) for letter in letters for bit in range(each)]

    def piece(self):
        core = lax.axis_index("core")
        chip = self.chip()
        step_u = 1 + core * (self.depth - 1)
        step_v = self.depth - core * (self.depth - 1)
        return lambda u, v: jnp.bitwise_xor(chip, u * step_u + v * step_v)

    def array(self):
        return ((2 * self.rows // self.depth, LANES), F32)

    def whole(self):
        return ((2 * self.rows, LANES), F32)

    def place(self, form, refs, u, v):
        index, inner = {
            "u": (u, v),
            "v": (v, u),
            "all": (0, u * self.depth + v),
            "other": (0, v * self.depth + u),
        }[form]
        return refs[index], inner * 2 * self.part


def angle_pair(angles, which):
    return half_angle(jnp.broadcast_to(angles[0:1, which : which + 1], (TILE, LANES)))


def butterflies(real, imag, pair, bits):
    sine, cosine = pair
    tangent = sine / cosine
    scale = cosine
    for _ in bits[1:]:
        scale = scale * cosine
    for bit in bits:
        for first in range(len(real)):
            other = first | (1 << bit)
            if other == first:
                continue
            ar, ai, br, bi = real[first], imag[first], real[other], imag[other]
            real[first], imag[first] = ar - tangent * bi, ai + tangent * br
            real[other], imag[other] = br - tangent * ai, bi + tangent * ar
    return [scale * v for v in real], [scale * v for v in imag]


def flip_sum(values, index):
    total = None
    stride = 1
    while stride < len(values):
        term = values[index ^ stride]
        total = term if total is None else total + term
        stride *= 2
    return total


def load_slots(shape, form, refs, start, slots):
    real, imag = [], []
    for slot in slots:
        ref, base = shape.place(form, refs, *slot)
        real.append(ref[base + start : base + start + TILE, :])
        imag.append(ref[base + shape.part + start : base + shape.part + start + TILE, :])
    return real, imag


def store_slots(shape, form, refs, start, slots, real, imag):
    for slot, re, im in zip(slots, real, imag):
        ref, base = shape.place(form, refs, *slot)
        ref[base + start : base + start + TILE, :] = re
        ref[base + shape.part + start : base + shape.part + start + TILE, :] = im


def load_planes(shape, form, refs):
    planes = []
    for u in range(shape.depth):
        pairs = []
        for v in range(shape.depth):
            ref, base = shape.place(form, refs, u, v)
            middle = base + shape.part
            pairs.append(jnp.concatenate([ref[base:middle, :], ref[middle : middle + shape.part, :]], axis=1))
        planes.append(jnp.concatenate(pairs, axis=0))
    return planes


def store_planes(shape, form, refs, planes):
    for u, v in shape.slots():
        re, im = planes[u]
        at = v * shape.part
        ref, base = shape.place(form, refs, u, v)
        middle = base + shape.part
        ref[base:middle, :] = re[at : at + shape.part]
        ref[middle : middle + shape.part, :] = im[at : at + shape.part]


def phased(real, imag, cosine, sine):
    return real * cosine - imag * sine, imag * cosine + real * sine


def load_raw(ref, base):
    return ref[pl.ds(base, TILE, stride=2), :], ref[pl.ds(base + 1, TILE, stride=2), :]


def first_rotations(shape, angle, raw, outs):
    piece = shape.piece()
    pair = angle_pair(angle, 3)
    for start in range(0, shape.part, TILE):
        for v in range(shape.depth):
            slots = [(u, v) for u in range(shape.depth)]
            parts = [load_raw(raw, (piece(*slot) * shape.part + start) * 2) for slot in slots]
            real, imag = butterflies([p[0] for p in parts], [p[1] for p in parts], pair, shape.bits("v"))
            store_slots(shape, "u", outs, start, slots, real, imag)


COPIES = 4


def pre_near(shape, angles, psi, lam):
    step = 2 * shape.rows // COPIES

    def body(angle, psi_ref, lam_ref, own, send, *rest):
        outs, angle_here, sems = rest[:-2], rest[-2], rest[-1]
        fetch = pltpu.make_async_copy(angle, angle_here, sems.at[2 * COPIES])
        fetch.start()

        def copies(own_ref, send_ref):
            pairs = [(own_ref, own, 0), (send_ref, send, COPIES)]
            return [
                pltpu.make_async_copy(
                    source.at[pl.ds(i * step, step), :], target.at[pl.ds(i * step, step), :], sems.at[first + i]
                )
                for source, target, first in pairs
                for i in range(COPIES)
            ]

        @pl.when(lax.axis_index("core") == 0)
        def _():
            for copy in copies(psi_ref, lam_ref):
                copy.start()

        @pl.when(lax.axis_index("core") != 0)
        def _():
            for copy in copies(lam_ref, psi_ref):
                copy.start()

        waits = copies(psi_ref, lam_ref)
        fetch.wait()
        for copy in waits[:COPIES]:
            copy.wait()
        first_rotations(shape, angle_here, own, outs)
        for copy in waits[COPIES:]:
            copy.wait()

    shapes = [shape.whole()] * 2 + [shape.array()] * shape.depth
    out = pl.pallas_call(
        body,
        name="pre_near",
        out_shape=[jax.ShapeDtypeStruct(size, kind) for size, kind in shapes],
        in_specs=[pl.BlockSpec(memory_space=pltpu.HBM)] * 3,
        out_specs=[pl.BlockSpec(memory_space=pltpu.VMEM)] * len(shapes),
        scratch_shapes=[pltpu.VMEM(angles.shape, F32), pltpu.SemaphoreType.DMA((2 * COPIES + 1,))],
        compiler_params=pltpu.CompilerParams(vmem_limit_bytes=VMEM_FIRST),
    )(angles, psi, lam)
    return out[0], out[1], out[2:]


def pre_far(shape, angles, raw):
    def body(angle, ref, *outs):
        first_rotations(shape, angle, ref, outs)

    return vmem_call("pre_far", body, [shape.array()] * shape.depth, inputs=(angles, raw))


def rotate_local(shape, angles, arrays, form, new_form, mats, which, hold=()):
    count = len(arrays)

    def body(*refs):
        matrices = [m[...] for m in refs[1 + count : 5 + count]]
        sine, cosine = half_angle(refs[0][0:1, which : which + 1])
        planes = load_planes(shape, form, refs[1 : 1 + count])
        store_planes(shape, new_form, refs[5 + count :], rotate_all(planes, *matrices, cosine, sine))

    return vmem_call(
        "rotate_local",
        body,
        [shape.array()] * shape.depth,
        inputs=(angles,) + tuple(arrays) + tuple(mats),
        hold=hold,
    )


def halves(shape, ref):
    size = 2 * shape.rows
    return [ref.at[pl.ds(i * size, size), :] for i in range(2)]


def turn(shape, angles, near, far, field_b):
    size = shape.depth

    def body(*refs):
        states = refs[1 : 1 + size], refs[1 + size : 1 + 2 * size]
        cos_b, sin_b = refs[1 + 2 * size : 3 + 2 * size]
        before = halves(shape, refs[3 + 2 * size])
        outs = refs[4 + 2 * size : 4 + 3 * size], refs[4 + 3 * size :]
        pair_one, pair_zero = angle_pair(refs[0], 3), angle_pair(refs[0], 1)
        bits = list(range(size.bit_length()))
        for start in range(0, shape.part, TILE):
            for u in range(size):
                slots = [(u, v) for v in range(size)]
                real, imag = load_slots(shape, "v", states[0], start, slots)
                far_real, far_imag = load_slots(shape, "v", states[1], start, slots)
                real, imag = butterflies(real + far_real, imag + far_imag, pair_one, bits)
                store_slots(shape, "all", before[:1], start, slots, real[:size], imag[:size])
                store_slots(shape, "all", before[1:], start, slots, real[size:], imag[size:])
                for i in range(2 * size):
                    row = (i // size) * shape.rows + (u * size + i % size) * shape.part + start
                    real[i], imag[i] = phased(
                        real[i], imag[i], cos_b[row : row + TILE, :], sin_b[row : row + TILE, :]
                    )
                real, imag = butterflies(real, imag, pair_zero, bits)
                store_slots(shape, "v", outs[0], start, slots, real[:size], imag[:size])
                store_slots(shape, "v", outs[1], start, slots, real[size:], imag[size:])

    result = vmem_call(
        "turn",
        body,
        [((4 * shape.rows, LANES), F32)] + [shape.array()] * (2 * size),
        inputs=(angles,) + tuple(near) + tuple(far) + (field_b[1], field_b[2]),
    )
    return result[0], result[1 : 1 + size], result[1 + size :]


def flip_raw(shape, own, other, hold=()):
    pieces = shape.rows // shape.part

    def body(own_ref, other_ref, out):
        total = jnp.zeros((TILE, LANES), F32)
        for start in range(0, shape.part, TILE):
            parts = [load_raw(own_ref, (i * shape.part + start) * 2) for i in range(pieces)]
            own_re, own_im = [p[0] for p in parts], [p[1] for p in parts]
            for i in range(pieces):
                other_re, other_im = load_raw(other_ref, (i * shape.part + start) * 2)
                total = total + other_re * flip_sum(own_im, i) - other_im * flip_sum(own_re, i)
        out[...] = sign(jnp.sum(total, axis=0, keepdims=True))

    return vmem_call("flip_raw", body, [((1, LANES), F32)], inputs=(own, other), hold=hold)[0]


def sign(value):
    return jnp.where(lax.axis_index("core") == 0, value, -value)


def flip_mats(low):
    small = flip_mat(LANES)
    zero = jnp.zeros_like(small)
    lane_flip = jnp.concatenate(
        [jnp.concatenate([small, zero], axis=1), jnp.concatenate([zero, small], axis=1)], axis=0
    )
    return lane_flip, flip_mat(low)


def gradients_mid(shape, field_b, own_before, other_before):
    low = shape.low

    def body(cost, cos_b, sin_b, own_ref, other_ref, out):
        lane_flip, row_flip = flip_mats(low)

        def turned(block, row):
            re, im = phased(
                block[:, :LANES], block[:, LANES:], cos_b[row : row + low, :], sin_b[row : row + low, :]
            )
            return jnp.concatenate([re, im], axis=1)

        near, far = (load_planes(shape, "all", [ref]) for ref in halves(shape, own_ref))
        other_far, other = (load_planes(shape, "other", [ref]) for ref in halves(shape, other_ref))
        inter = jnp.zeros((1, LANES), F32)
        mix_one = jnp.zeros((1, LANES), F32)
        mix_zero = jnp.zeros((1, LANES), F32)
        for u, flips in enumerate(flips_all(near, lane_flip, row_flip)):
            mix_one = mix_one + cross_imag(other[u], flips + 0.5 * far[u]) + cross_imag(other_far[u], 0.5 * near[u])
            weight = cost[u * low : (u + 1) * low, :]
            inter = inter + cross_imag(other[u], jnp.concatenate([weight] * 2, axis=1) * near[u])
        near = [turned(block, u * low) for u, block in enumerate(near)]
        for u, flips in enumerate(flips_all(near, lane_flip, row_flip)):
            across = 0.5 * turned(far[u], shape.rows + u * low)
            mix_zero = mix_zero + cross_imag(turned(other[u], u * low), flips + across)
            mix_zero = mix_zero + cross_imag(turned(other_far[u], shape.rows + u * low), 0.5 * near[u])
        out[...] = sign(jnp.concatenate([mix_zero, inter, mix_one], axis=0))

    return vmem_call(
        "gradients_mid", body, [((3, LANES), F32)], inputs=tuple(field_b) + (own_before, other_before)
    )[0]


def post_send(shape, angles, arrays, hold=()):
    count = len(arrays)

    def body(*refs):
        pair = angle_pair(refs[0], 1)
        for start in range(0, shape.part, TILE):
            for v in range(shape.depth):
                slots = [(u, v) for u in range(shape.depth)]
                real, imag = load_slots(shape, "u", refs[1 : 1 + count], start, slots)
                real, imag = butterflies(real, imag, pair, shape.bits("v"))
                store_slots(shape, "all", [refs[1 + count]], start, slots, real, imag)

    return vmem_call("post_send", body, [shape.whole()], inputs=(angles,) + tuple(arrays), hold=hold)[0]


def flips_other(shape, other):
    def body(ref, out):
        slots = shape.slots()
        for start in range(0, shape.part, TILE):
            real, imag = load_slots(shape, "other", [ref], start, slots)
            flips = [[flip_sum(values, i) for i in range(len(slots))] for values in (real, imag)]
            store_slots(shape, "all", [out], start, slots, *flips)

    return vmem_call("flips_other", body, [shape.whole()], inputs=(other,))[0]


def post_grads(shape, angles, arrays, other, flips, cost_a, hold=()):
    count = len(arrays)

    def body(*refs):
        other_ref, flips_ref, cost = refs[1 + count : 4 + count]
        mixed, out = refs[4 + count :]
        piece = shape.piece()
        pair = angle_pair(refs[0], 1)
        mix = jnp.zeros((TILE, LANES), F32)
        inter = jnp.zeros((TILE, LANES), F32)
        for start in range(0, shape.part, TILE):
            for v in range(shape.depth):
                slots = [(u, v) for u in range(shape.depth)]
                real, imag = load_slots(shape, "u", refs[1 : 1 + count], start, slots)
                real, imag = butterflies(real, imag, pair, shape.bits("v"))
                store_slots(shape, "all", [mixed], start, slots, real, imag)
                other_re, other_im = load_slots(shape, "other", [other_ref], start, slots)
                flip_re, flip_im = load_slots(shape, "all", [flips_ref], start, slots)
                for i, slot in enumerate(slots):
                    mix = mix + flip_re[i] * imag[i] - flip_im[i] * real[i]
                    row = pl.multiple_of(piece(*slot) * shape.part + start, TILE)
                    value = cost[pl.ds(row, TILE), :]
                    inter = inter + value * (other_re[i] * imag[i] - other_im[i] * real[i])
        out[0:1, :] = sign(jnp.sum(inter, axis=0, keepdims=True))
        out[1:2, :] = sign(jnp.sum(mix, axis=0, keepdims=True))

    return vmem_call(
        "post_grads",
        body,
        [shape.whole(), ((2, LANES), F32)],
        inputs=(angles,) + tuple(arrays) + (other, flips, cost_a),
        hold=hold,
    )


def post_phase(shape, mixed, other, field_a):
    def body(own_ref, other_ref, cos_a, sin_a, psi_out, lam_out):
        first = lax.axis_index("core") == 0
        piece = shape.piece()
        slots = shape.slots()
        for start in range(0, shape.part, TILE):
            own_re, own_im = load_slots(shape, "all", [own_ref], start, slots)
            other_re, other_im = load_slots(shape, "other", [other_ref], start, slots)
            for i, slot in enumerate(slots):
                row = pl.multiple_of(piece(*slot) * shape.part + start, TILE)
                cosine, sine = cos_a[pl.ds(row, TILE), :], sin_a[pl.ds(row, TILE), :]
                own_pair = phased(own_re[i], own_im[i], cosine, sine)
                other_pair = phased(other_re[i], other_im[i], cosine, sine)
                for j in range(2):
                    span = pl.ds(2 * row + j, TILE, stride=2)
                    psi_out[span, :] = jnp.where(first, own_pair[j], other_pair[j])
                    lam_out[span, :] = jnp.where(first, other_pair[j], own_pair[j])

    return vmem_call(
        "post_phase", body, [shape.whole()] * 2, inputs=(mixed, other, field_a[1], field_a[2])
    )


AXES = ("grp", "z", "core")


def swap_cores(array):
    return lax.ppermute(array, "core", [(0, 1), (1, 0)])


def swap(shape, arrays, form):
    size = shape.depth
    out = list(arrays)
    with jax.named_scope("exchange_" + form):
        for i in sorted(range(1, size), key=lambda i: (i.bit_count() == 1, -i)):
            pairs = []
            for chip in range(size * size):
                for core in range(CORES):
                    step = i if (core == 0) == (form == "u") else i * size
                    pairs.append((chip * CORES + core, (chip ^ step) * CORES + core))
            out[i] = lax.ppermute(arrays[i], AXES, pairs)
    return out


def total_grads(shape, parts):
    def join(early, mid_part, late, out):
        rows = [late[0:1, :], late[1:2, :] + mid_part[0:1, :], mid_part[1:2, :], mid_part[2:3, :] + early[...]]
        out[...] = jnp.concatenate(rows + [jnp.zeros((TILE - 4, LANES), F32)], axis=0)

    def add(*refs):
        values = [ref[...] for ref in refs[:-1]]
        while len(values) > 1:
            values = [left + right for left, right in zip(values[::2], values[1::2])]
        refs[-1][...] = values[0]

    block_shape = [((TILE, LANES), F32)]
    block = vmem_call("join_grads", join, block_shape, inputs=tuple(parts))[0]
    for axis, size in (("core", CORES), ("grp", shape.groups), ("z", shape.depth)):
        stride = 1
        while stride < size:
            reach = min(4, size // stride)
            others = [
                lax.ppermute(block, axis, [(j, j ^ (stride * i)) for j in range(size)]) for i in range(1, reach)
            ]
            block = vmem_call("add_grads", add, block_shape, inputs=(block, *others))[0]
            stride *= reach
    scale = 2.0 / (shape.rows * LANES * shape.devices)

    def finish(ref, out):
        summed = jnp.sum(ref[...], axis=1, keepdims=True) * scale
        for i in range(2 * LAYERS):
            out[i] = jnp.sum(summed[i : i + 1, :])

    return vmem_call("finish_grads", finish, [((2 * LAYERS,), F32)], inputs=(block,), smem_out=True)[0]


def after(values, first):
    return lax.optimization_barrier((values, first))[0]


def piece_mix(shape, angles, which, state):
    low = shape.low
    least = shape.part.bit_length() - 1

    def body(angle, ref, mixed, flipped):
        sine, cosine = half_angle(angle[0:1, which : which + 1])
        real, imag = mixer_mats(low, cosine, sine, least)
        row_high, row_low = split(jnp.concatenate([real, imag], axis=0))
        row_flip = flip_mat(low, least)
        blocks = [ref[i * low : (i + 1) * low, :] for i in range(shape.planes)]
        for i, (re, im) in enumerate(rotate_all(blocks, None, None, row_high, row_low, cosine, sine)):
            mixed[i * low : (i + 1) * low, :LANES] = re
            mixed[i * low : (i + 1) * low, LANES:] = im
        for i, block in enumerate(flips_all(blocks, None, row_flip)):
            flipped[i * low : (i + 1) * low, :] = block

    return vmem_call(
        "piece_mix",
        body, [((shape.rows, 2 * LANES), F32)] * 2, inputs=(angles, state,)
    )


def plain_cross(lam, other):
    def body(lam_ref, other_ref, out):
        out[...] = cross_imag(lam_ref[...], other_ref[...])

    return vmem_call("plain_cross", body, [((1, LANES), F32)], inputs=(lam, other))[0]


def plain_gradients(shape, field_b, psi_before, lam_before):
    low = shape.low

    def body(cost, cos_b, sin_b, psi_ref, lam_ref, out):
        lane_flip, row_flip = flip_mats(low)
        spans = [slice(i * low, (i + 1) * low) for i in range(shape.planes)]
        psi = [psi_ref[span, :] for span in spans]
        lam = [lam_ref[span, :] for span in spans]
        inter = jnp.zeros((1, LANES), F32)
        mix_one = jnp.zeros((1, LANES), F32)
        mix_zero = jnp.zeros((1, LANES), F32)
        for i, flips in enumerate(flips_all(psi, lane_flip, row_flip)):
            mix_one = mix_one + cross_imag(lam[i], flips)
            inter = inter + cross_imag(lam[i], jnp.concatenate([cost[spans[i], :]] * 2, axis=1) * psi[i])

        def turned(block, span):
            re, im = phased(block[:, :LANES], block[:, LANES:], cos_b[span, :], sin_b[span, :])
            return jnp.concatenate([re, im], axis=1)

        psi = [turned(block, span) for block, span in zip(psi, spans)]
        for i, flips in enumerate(flips_all(psi, lane_flip, row_flip)):
            mix_zero = mix_zero + cross_imag(turned(lam[i], spans[i]), flips)
        out[...] = jnp.concatenate([mix_zero, inter, mix_one], axis=0)

    return vmem_call("plain_gradients", body, [((3, LANES), F32)], inputs=tuple(field_b) + (psi_before, lam_before))[0]


def plain_phase(shape, state, field, gradient):
    def body(ref, cost, cosine, sine, out):
        real, imag = ref[:, :LANES], ref[:, LANES:]
        if gradient:
            re, im = cost[...] * real, cost[...] * imag
        else:
            re, im = phased(real, imag, cosine[...], sine[...])
        out[:, :LANES] = re
        out[:, LANES:] = im

    return vmem_call("plain_phase", body, [((shape.rows, 2 * LANES), F32)], inputs=(state,) + tuple(field))[0]


def mid_math(shape, angles, planes, mats, cos_b, sin_b):
    low = shape.low
    sine, cosine = half_angle(angles[0:1, 3:4])
    first = rotate_all(planes, *[m[...] for m in mats[4:8]], cosine, sine)
    turned = []
    for i, (re, im) in enumerate(first):
        re, im = phased(re, im, cos_b[i * low : (i + 1) * low, :], sin_b[i * low : (i + 1) * low, :])
        turned.append(jnp.concatenate([re, im], axis=1))
    sine, cosine = half_angle(angles[0:1, 1:2])
    second = rotate_all(turned, *[m[...] for m in mats[0:4]], cosine, sine)
    return first, second


def plain_mid(shape, angles, state, field_b, mats):
    low = shape.low

    def body(angle, ref, cos_b, sin_b, *rest):
        blocks = [ref[i * low : (i + 1) * low, :] for i in range(shape.planes)]
        for out, pairs in zip(rest[8:], mid_math(shape, angle, blocks, rest[:8], cos_b, sin_b)):
            for i, (re, im) in enumerate(pairs):
                out[i * low : (i + 1) * low, :LANES] = re
                out[i * low : (i + 1) * low, LANES:] = im

    return vmem_call(
        "plain_mid",
        body,
        [((shape.rows, 2 * LANES), F32)] * 2,
        inputs=(angles, state, field_b[1], field_b[2]) + tuple(mats[0]) + tuple(mats[1]),
    )


def exchange_all(shape, state):
    block = state.reshape(shape.devices, -1, 2 * LANES)
    return lax.all_to_all(block, AXES, 0, 0, tiled=True).reshape(state.shape)


def plain(shape, forward, adjoint, edges, weights, layout, slab_bits, angles):
    rows = shape.rows

    def wide(array):
        return array.reshape(2, rows, LANES).transpose(1, 0, 2).reshape(rows, 2 * LANES)

    def narrow(array):
        return array.reshape(rows, 2, LANES).transpose(1, 0, 2).reshape(2, rows * LANES)

    def before(row):
        return shape.own() * rows + row

    def beyond(row):
        return (row // shape.part) * rows + shape.own() * shape.part + row % shape.part

    angles = angles.reshape(1, -1)
    small = small_inputs(edges, weights, layout, slab_bits)
    fields = make_fields(angles, *small, (rows, rows), before, beyond, shape.known)
    field_a, field_b = fields[:3], fields[3:]
    mats = make_mats(angles, shape.low)
    psi, flips = piece_mix(shape, angles, 3, wide(forward))
    lam, _ = piece_mix(shape, angles, 3, wide(adjoint))
    early = plain_cross(wide(adjoint), flips)
    psi_before, psi_after = plain_mid(shape, angles, exchange_all(shape, psi), field_b, mats)
    lam_before, lam_after = plain_mid(shape, angles, exchange_all(shape, lam), field_b, mats)
    mid_part = plain_gradients(shape, field_b, psi_before, lam_before)
    psi, lam = exchange_all(shape, psi_after), exchange_all(shape, lam_after)
    psi_mixed, flips = piece_mix(shape, angles, 1, psi)
    lam_mixed, _ = piece_mix(shape, angles, 1, lam)
    late = jnp.concatenate(
        [plain_cross(lam_mixed, plain_phase(shape, psi_mixed, field_a, True)), plain_cross(lam, flips)], axis=0
    )
    grads = total_grads(shape, (early, mid_part, late))
    outs = [narrow(plain_phase(shape, state, field_a, False)) for state in (psi_mixed, lam_mixed)]
    return outs[0], outs[1], grads


def interleave(array, rows):
    return array.reshape(2, rows, LANES).transpose(1, 0, 2).reshape(2 * rows, LANES)


def deinterleave(array, rows):
    return array.reshape(rows, 2, LANES).transpose(1, 0, 2).reshape(2, rows * LANES)


def places(shape):
    def before(row):
        return shape.own() * shape.rows + row

    def beyond(row):
        far, slot, inner = row // shape.rows, (row % shape.rows) // shape.part, row % shape.part
        source = shape.piece()(slot // shape.depth, slot % shape.depth) * CORES
        source = source + jnp.bitwise_xor(lax.axis_index("core"), far)
        return source * shape.rows + shape.chip() * shape.part + inner

    return before, beyond


def pipelined(shape, forward, adjoint, edges, weights, layout, slab_bits, angles):
    rows = shape.rows
    angles = angles.reshape(1, -1)
    own_raw, other_raw, near = pre_near(shape, angles, interleave(forward, rows), interleave(adjoint, rows))
    far_raw = swap_cores(other_raw)
    mats = make_mats(angles, shape.low, hold=near[:1])
    before, beyond = places(shape)
    small = small_inputs(edges, weights, layout, slab_bits)
    sizes = (rows, 2 * rows), before, beyond, shape.known
    fields = make_fields(angles, *small, *sizes, core=1, hold=near[:1])
    near = swap(shape, near, "u")
    far = swap(shape, pre_far(shape, angles, far_raw), "u")
    near = swap(shape, rotate_local(shape, angles, near, "u", "v", mats[1], 3, hold=fields[:1]), "v")
    far = rotate_local(shape, angles, far, "u", "v", mats[1], 3)
    fields = make_fields(angles, *small, *sizes, core=0, hold=after(fields, far[0]))
    field_a, field_b = fields[:3], fields[3:]
    early = flip_raw(shape, own_raw, other_raw, hold=far[:1])
    far = swap(shape, far, "v")
    own_before, near, far = turn(shape, angles, near, far, field_b)
    far = swap(shape, far, "v")
    near = swap(shape, near, "v")
    other_before = swap_cores(own_before)
    far = swap(shape, rotate_local(shape, angles, far, "v", "u", mats[0], 1), "u")
    near = rotate_local(shape, angles, near, "v", "u", mats[0], 1)
    other = swap_cores(post_send(shape, angles, far, hold=near[:1]))
    near = swap(shape, near, "u")
    mid_part = gradients_mid(shape, field_b, own_before, other_before)
    flips = flips_other(shape, other)
    mixed, late = post_grads(shape, angles, near, other, flips, field_a[0], hold=(mid_part, early))
    grads = total_grads(shape, (early, mid_part, late))
    psi_out, lam_out = post_phase(shape, mixed, other, field_a)
    return deinterleave(psi_out, rows), deinterleave(lam_out, rows), grads


def solution(mesh):
    groups, rest = mesh.shape["grp"], mesh.shape["rep"]
    depth = rest // CORES
    fine = Mesh(mesh.devices.reshape(groups, depth, CORES), AXES)

    def per_device(forward, *others):
        shape = Shape(groups, depth, forward.shape[1])
        return (pipelined if shape.tiles else plain)(shape, forward, *others)

    state = P(None, AXES)
    return jax.shard_map(
        per_device,
        mesh=fine,
        in_specs=(state, state, P(), P(), P(), P(), P()),
        out_specs=(state, state, P()),
        check_vma=False,
    )
```

```python
import jax
import jax.numpy as jnp
from jax import lax
from jax.experimental import pallas as pl
from jax.experimental.pallas import tpu as pltpu
from jax.sharding import Mesh, PartitionSpec as P

NODES = 40
LAYERS = 2
LANES = 128
TILE = 8
CORES = 2
F32 = jnp.float32
BF16 = jnp.bfloat16
VMEM_LIMIT = 12 << 20
PIECES = 4
VMEM_FIRST = 52 << 20


def vmem_call(name, body, out_shapes, inputs=(), smem_out=False, hold=()):
    if hold:
        taken = len(inputs)
        inner = body

        def body(*refs):
            inner(*refs[:taken], *refs[taken + len(hold) :])

        inputs = tuple(inputs) + tuple(hold)
    specs = [pl.BlockSpec(memory_space=pltpu.VMEM)] * len(inputs)
    place = pltpu.SMEM if smem_out else pltpu.VMEM
    return pl.pallas_call(
        body,
        name=name,
        out_shape=[jax.ShapeDtypeStruct(shape, kind) for shape, kind in out_shapes],
        in_specs=specs,
        out_specs=[pl.BlockSpec(memory_space=place)] * len(out_shapes),
        compiler_params=pltpu.CompilerParams(vmem_limit_bytes=VMEM_LIMIT),
    )(*inputs)


def half_angle(x):
    y = 0.5 * x
    z = y * y
    sin_y = jnp.full_like(z, -1.0 / 1307674368000.0)
    for factor in (6227020800.0, -39916800.0, 362880.0, -5040.0, 120.0, -6.0, 1.0):
        sin_y = sin_y * z + 1.0 / factor
    sin_y = sin_y * y
    cos_y = jnp.full_like(z, 1.0 / 20922789888000.0)
    for factor in (-87178291200.0, 479001600.0, -3628800.0, 40320.0, -720.0, 24.0, -2.0, 1.0):
        cos_y = cos_y * z + 1.0 / factor
    return 2.0 * sin_y * cos_y, 1.0 - 2.0 * sin_y * sin_y


def split(value):
    high = value.astype(BF16)
    return high, (value - high.astype(F32)).astype(BF16)


def dot(left, right):
    return jnp.dot(left, right, preferred_element_type=F32)


def mixer_mats(size, cos_beta, sin_beta, least=0):
    row = lax.broadcasted_iota(jnp.int32, (size, size), 0)
    col = lax.broadcasted_iota(jnp.int32, (size, size), 1)
    differ = jnp.bitwise_xor(row, col)
    real = jnp.ones((size, size), F32)
    real = jnp.where(jnp.bitwise_and(differ, (1 << least) - 1) == 0, real, 0.0)
    imag = jnp.zeros((size, size), F32)
    for bit in range(least, size.bit_length() - 1):
        flagged = jnp.bitwise_and(differ, 1 << bit) != 0
        real, imag = (
            jnp.where(flagged, -imag * sin_beta, real * cos_beta),
            jnp.where(flagged, real * sin_beta, imag * cos_beta),
        )
    return real, imag


def flip_mat(size, least=0):
    row = lax.broadcasted_iota(jnp.int32, (size, size), 0)
    col = lax.broadcasted_iota(jnp.int32, (size, size), 1)
    differ = jnp.bitwise_xor(row, col)
    count = jnp.zeros((size, size), jnp.int32)
    for bit in range(size.bit_length() - 1):
        count = count + jnp.bitwise_and(differ >> bit, 1)
    rest = jnp.bitwise_and(differ, (1 << least) - 1)
    return jnp.where(jnp.logical_and(count == 1, rest == 0), 1.0, 0.0).astype(BF16)


def rotate_all(planes, lane_high, lane_low, row_high, row_low, cos_beta, sin_beta):
    low = planes[0].shape[0]
    mixed = []
    for block in planes:
        high, rest = split(block)
        if lane_high is not None:
            lanes = dot(high, lane_high) + dot(rest, lane_high) + dot(high, lane_low)
            high, rest = split(lanes)
        both = dot(row_high, high) + dot(row_high, rest) + dot(row_low, high)
        real = both[:low, :LANES] - both[low:, LANES:]
        imag = both[:low, LANES:] + both[low:, :LANES]
        mixed.append((real, imag))
    stride = 1
    while stride < len(mixed):
        for first in range(len(mixed)):
            if first & stride:
                continue
            (ar, ai), (br, bi) = mixed[first], mixed[first + stride]
            mixed[first] = (cos_beta * ar - sin_beta * bi, cos_beta * ai + sin_beta * br)
            mixed[first + stride] = (cos_beta * br - sin_beta * ai, cos_beta * bi + sin_beta * ar)
        stride *= 2
    return mixed


def flips_all(planes, lane_flip, row_flip):
    out = []
    for index, block in enumerate(planes):
        high, rest = split(block)
        total = dot(row_flip, high) + dot(row_flip, rest)
        if lane_flip is not None:
            total = total + dot(high, lane_flip) + dot(rest, lane_flip)
        stride = 1
        while stride < len(planes):
            total = total + planes[index ^ stride]
            stride *= 2
        out.append(total)
    return out


def fold_rows(value):
    folded = value[:TILE]
    for start in range(TILE, value.shape[0], TILE):
        folded = folded + value[start : start + TILE]
    return jnp.sum(folded, axis=0, keepdims=True)


def cross_imag(lam, other):
    return fold_rows(lam[:, :LANES] * other[:, LANES:] - lam[:, LANES:] * other[:, :LANES])


def spin_rows(position, layout, slab, known):
    lane_bits = LANES.bit_length() - 1
    shift = jnp.clip(layout - lane_bits, 0, known - 1)
    inside = jnp.bitwise_and(jnp.right_shift(position, shift), 1)
    bit = jnp.where(layout < known + lane_bits, inside, slab)
    return jnp.where(layout < lane_bits, 0, 1 - 2 * bit).astype(F32)


def field_body(place_first, place_second, known):
    lane_bits = LANES.bit_length() - 1

    def body(angles, edges, weights, layout, slab, cost_a, cos_a, sin_a, cost_b, cos_b, sin_b):
        node = lax.broadcasted_iota(jnp.int32, (NODES, edges.shape[1]), 0)
        first = jnp.where(edges[0:1, :] == node, 1.0, 0.0)
        second = jnp.where(edges[1:2, :] == node, 1.0, 0.0)
        weight = weights[...].astype(F32)
        total = jnp.sum(weight, axis=1, keepdims=True)
        exact = lax.Precision.HIGHEST

        def full(left, right, dims):
            return lax.dot_general(left, right, dims, precision=exact, preferred_element_type=F32)

        plain = (((1,), (0,)), ((), ()))
        turned = (((1,), (1,)), ((), ()))
        matrix = full(first * weight, second, turned) + full(second * weight, first, turned)
        lane = lax.broadcasted_iota(jnp.int32, (LANES, NODES), 0)
        lane_layout = layout[...]
        lane_bit = jnp.bitwise_and(jnp.right_shift(lane, jnp.clip(lane_layout, 0, lane_bits - 1)), 1)
        lane_spin = jnp.where(lane_layout < lane_bits, 1 - 2 * lane_bit, 0).astype(F32)
        lane_energy = full(jnp.ones((TILE, NODES), F32), lane_spin * full(lane_spin, matrix, plain), turned)[0:1]

        def field(position, cost, cos_out, sin_out, gamma):
            spins = spin_rows(position, lane_layout, slab[...], known)
            pulled = full(spins, matrix, plain)
            energy = jnp.sum(pulled * spins, axis=1, keepdims=True)
            energy = energy + lane_energy + 2.0 * full(pulled, lane_spin, turned)
            value = 2.0 - energy / total
            cost[...] = value
            sine, cosine = half_angle(gamma * value)
            cos_out[...] = cosine
            sin_out[...] = sine

        row = lax.broadcasted_iota(jnp.int32, (cost_a.shape[0], 1), 0)
        field(place_first(row), cost_a, cos_a, sin_a, angles[0:1, 0:1])
        row = lax.broadcasted_iota(jnp.int32, (cost_b.shape[0], 1), 0)
        field(place_second(row), cost_b, cos_b, sin_b, angles[0:1, 2:3])
    return body


def make_fields(angles, edges, weights, layout, slab, rows, place_first, place_second, known, core=None, hold=()):
    inner = field_body(place_first, place_second, known)
    shapes = [((rows[0], LANES), F32)] * 3 + [((rows[1], LANES), F32)] * 3
    small = (angles, edges, weights, layout, slab)
    held = tuple(hold)

    def body(*refs):
        refs = refs[: len(small)] + refs[len(small) + len(held) :]
        if core is None:
            inner(*refs)
        else:

            @pl.when(lax.axis_index("core") == core)
            def _():
                inner(*refs)

    return pl.pallas_call(
        body,
        name="make_fields",
        out_shape=[jax.ShapeDtypeStruct(size, kind) for size, kind in shapes],
        in_specs=[pl.BlockSpec(memory_space=pltpu.VMEM)] * (len(small) + len(held)),
        out_specs=[pl.BlockSpec(memory_space=pltpu.VMEM)] * len(shapes),
        input_output_aliases={len(small) + i: i for i in range(len(shapes))} if len(held) == len(shapes) else {},
        compiler_params=pltpu.CompilerParams(vmem_limit_bytes=VMEM_LIMIT),
    )(*small, *held)


def make_mats(angles, low, hold=()):
    def body(angles, *mats):
        for layer in range(LAYERS):
            sine, cosine = half_angle(angles[0:1, 2 * layer + 1 : 2 * layer + 2])
            real, imag = mixer_mats(LANES, cosine, sine)
            lanes = jnp.concatenate(
                [jnp.concatenate([real, imag], axis=1), jnp.concatenate([-imag, real], axis=1)], axis=0
            )
            mats[4 * layer][...], mats[4 * layer + 1][...] = split(lanes)
            real, imag = mixer_mats(low, cosine, sine)
            mats[4 * layer + 2][...], mats[4 * layer + 3][...] = split(jnp.concatenate([real, imag], axis=0))

    shapes = ([((2 * LANES, 2 * LANES), BF16)] * 2 + [((2 * low, low), BF16)] * 2) * LAYERS
    out = vmem_call("make_mats", body, shapes, inputs=(angles,), hold=hold)
    return [out[4 * layer : 4 + 4 * layer] for layer in range(LAYERS)]


def small_inputs(edges, weights, layout, slab_bits):
    return edges.T, weights.reshape(1, -1), layout.reshape(1, -1), slab_bits.reshape(1, -1)


class Shape:
    def __init__(self, groups, depth, amp_dev):
        self.groups = groups
        self.depth = depth
        self.devices = groups * depth * CORES
        self.rows = amp_dev // LANES
        self.known = (self.rows * self.devices).bit_length() - 1
        self.tiles = groups == depth and self.rows % (groups * depth * TILE) == 0
        self.part = self.rows // (groups * depth if self.tiles else self.devices)
        self.low = depth * self.part if self.tiles else min(self.rows, 2 * LANES)
        self.planes = self.rows // self.low
        self.batch = max(depth // PIECES, 1)

    def own(self):
        return self.chip() * CORES + lax.axis_index("core")

    def chip(self):
        return lax.axis_index("grp") * self.depth + lax.axis_index("z")

    def slots(self):
        return [(u, v) for u in range(self.depth) for v in range(self.depth)]

    def bits(self, letters):
        each = self.depth.bit_length() - 1
        return [bit + (each if letter == "u" else 0) for letter in letters for bit in range(each)]

    def piece(self):
        core = lax.axis_index("core")
        chip = self.chip()
        step_u = 1 + core * (self.depth - 1)
        step_v = self.depth - core * (self.depth - 1)
        return lambda u, v: jnp.bitwise_xor(chip, u * step_u + v * step_v)

    def array(self):
        return ((2 * self.rows // self.depth, LANES), F32)

    def whole(self):
        return ((2 * self.rows, LANES), F32)

    def place(self, form, refs, u, v):
        index, inner = {
            "u": (u, v),
            "v": (v, u),
            "all": (0, u * self.depth + v),
            "other": (0, v * self.depth + u),
            "part": (u // self.batch, u % self.batch * self.depth + v),
            "other_part": (v // self.batch, v % self.batch * self.depth + u),
        }[form]
        return refs[index], inner * 2 * self.part


def angle_pair(angles, which):
    return half_angle(jnp.broadcast_to(angles[0:1, which : which + 1], (TILE, LANES)))


def butterflies(real, imag, pair, bits):
    sine, cosine = pair
    tangent = sine / cosine
    scale = cosine
    for _ in bits[1:]:
        scale = scale * cosine
    for bit in bits:
        for first in range(len(real)):
            other = first | (1 << bit)
            if other == first:
                continue
            ar, ai, br, bi = real[first], imag[first], real[other], imag[other]
            real[first], imag[first] = ar - tangent * bi, ai + tangent * br
            real[other], imag[other] = br - tangent * ai, bi + tangent * ar
    return [scale * v for v in real], [scale * v for v in imag]


def flip_sum(values, index):
    total = None
    stride = 1
    while stride < len(values):
        term = values[index ^ stride]
        total = term if total is None else total + term
        stride *= 2
    return total


def sent_order(arrays):
    return tuple(arrays[2:]) + (arrays[1], arrays[0])


def plain_order(arrays):
    return (arrays[-1], arrays[-2]) + tuple(arrays[:-2])


def load_slots(shape, form, refs, start, slots):
    real, imag = [], []
    for slot in slots:
        ref, base = shape.place(form, refs, *slot)
        real.append(ref[base + start : base + start + TILE, :])
        imag.append(ref[base + shape.part + start : base + shape.part + start + TILE, :])
    return real, imag


def store_slots(shape, form, refs, start, slots, real, imag):
    for slot, re, im in zip(slots, real, imag):
        ref, base = shape.place(form, refs, *slot)
        ref[base + start : base + start + TILE, :] = re
        ref[base + shape.part + start : base + shape.part + start + TILE, :] = im


def load_planes(shape, form, refs):
    planes = []
    for u in range(shape.depth):
        pairs = []
        for v in range(shape.depth):
            ref, base = shape.place(form, refs, u, v)
            middle = base + shape.part
            pairs.append(jnp.concatenate([ref[base:middle, :], ref[middle : middle + shape.part, :]], axis=1))
        planes.append(jnp.concatenate(pairs, axis=0))
    return planes


def store_planes(shape, form, refs, planes):
    for u, v in shape.slots():
        re, im = planes[u]
        at = v * shape.part
        ref, base = shape.place(form, refs, u, v)
        middle = base + shape.part
        ref[base:middle, :] = re[at : at + shape.part]
        ref[middle : middle + shape.part, :] = im[at : at + shape.part]


def phased(real, imag, cosine, sine):
    return real * cosine - imag * sine, imag * cosine + real * sine


def load_raw(ref, base):
    return ref[pl.ds(base, TILE, stride=2), :], ref[pl.ds(base + 1, TILE, stride=2), :]


def first_rotations(shape, angle, raw, outs):
    piece = shape.piece()
    pair = angle_pair(angle, 3)
    for start in range(0, shape.part, TILE):
        for v in range(shape.depth):
            slots = [(u, v) for u in range(shape.depth)]
            parts = [load_raw(raw, (piece(*slot) * shape.part + start) * 2) for slot in slots]
            real, imag = butterflies([p[0] for p in parts], [p[1] for p in parts], pair, shape.bits("v"))
            store_slots(shape, "u", outs, start, slots, real, imag)


COPIES = 4


def pre_near(shape, angles, psi, lam):
    step = 2 * shape.rows // COPIES

    def body(angle, psi_ref, lam_ref, own, send, *rest):
        outs, angle_here, sems = rest[:-2], rest[-2], rest[-1]
        fetch = pltpu.make_async_copy(angle, angle_here, sems.at[2 * COPIES])
        fetch.start()

        def copies(own_ref, send_ref):
            pairs = [(own_ref, own, 0), (send_ref, send, COPIES)]
            return [
                pltpu.make_async_copy(
                    source.at[pl.ds(i * step, step), :], target.at[pl.ds(i * step, step), :], sems.at[first + i]
                )
                for source, target, first in pairs
                for i in range(COPIES)
            ]

        @pl.when(lax.axis_index("core") == 0)
        def _():
            for copy in copies(psi_ref, lam_ref):
                copy.start()

        @pl.when(lax.axis_index("core") != 0)
        def _():
            for copy in copies(lam_ref, psi_ref):
                copy.start()

        waits = copies(psi_ref, lam_ref)
        fetch.wait()
        for copy in waits[:COPIES]:
            copy.wait()
        first_rotations(shape, angle_here, own, outs)
        for copy in waits[COPIES:]:
            copy.wait()

    shapes = [shape.whole()] * 2 + [shape.array()] * shape.depth
    out = pl.pallas_call(
        body,
        name="pre_near",
        out_shape=[jax.ShapeDtypeStruct(size, kind) for size, kind in shapes],
        in_specs=[pl.BlockSpec(memory_space=pltpu.HBM)] * 3,
        out_specs=[pl.BlockSpec(memory_space=pltpu.VMEM)] * len(shapes),
        scratch_shapes=[pltpu.VMEM(angles.shape, F32), pltpu.SemaphoreType.DMA((2 * COPIES + 1,))],
        compiler_params=pltpu.CompilerParams(vmem_limit_bytes=VMEM_FIRST),
    )(angles, psi, lam)
    return out[0], out[1], out[2:]


def pre_far(shape, angles, raw):
    def body(angle, ref, *outs):
        first_rotations(shape, angle, ref, outs)

    return vmem_call("pre_far", body, [shape.array()] * shape.depth, inputs=(angles, raw))


def rotate_local(shape, angles, arrays, form, new_form, mats, which, hold=()):
    count = len(arrays)

    def body(*refs):
        matrices = [m[...] for m in refs[1 + count : 5 + count]]
        sine, cosine = half_angle(refs[0][0:1, which : which + 1])
        planes = load_planes(shape, form, plain_order(refs[1 : 1 + count]))
        store_planes(shape, new_form, refs[5 + count :], rotate_all(planes, *matrices, cosine, sine))

    return vmem_call(
        "rotate_local",
        body,
        [shape.array()] * shape.depth,
        inputs=(angles,) + sent_order(arrays) + tuple(mats),
        hold=hold,
    )


def halves(shape, ref):
    size = 2 * shape.rows
    return [ref.at[pl.ds(i * size, size), :] for i in range(2)]


def turn(shape, angles, near, far, field_b):
    size = shape.depth

    def body(*refs):
        states = plain_order(refs[1 : 1 + size]), plain_order(refs[1 + size : 1 + 2 * size])
        cos_b, sin_b = refs[1 + 2 * size : 3 + 2 * size]
        before = halves(shape, refs[3 + 2 * size])
        outs = refs[4 + 2 * size : 4 + 3 * size], refs[4 + 3 * size :]
        pair_one, pair_zero = angle_pair(refs[0], 3), angle_pair(refs[0], 1)
        bits = list(range(size.bit_length()))
        for start in range(0, shape.part, TILE):
            for u in range(size):
                slots = [(u, v) for v in range(size)]
                real, imag = load_slots(shape, "v", states[0], start, slots)
                far_real, far_imag = load_slots(shape, "v", states[1], start, slots)
                real, imag = butterflies(real + far_real, imag + far_imag, pair_one, bits)
                store_slots(shape, "all", before[:1], start, slots, real[:size], imag[:size])
                store_slots(shape, "all", before[1:], start, slots, real[size:], imag[size:])
                for i in range(2 * size):
                    row = (i // size) * shape.rows + (u * size + i % size) * shape.part + start
                    real[i], imag[i] = phased(
                        real[i], imag[i], cos_b[row : row + TILE, :], sin_b[row : row + TILE, :]
                    )
                real, imag = butterflies(real, imag, pair_zero, bits)
                store_slots(shape, "v", outs[0], start, slots, real[:size], imag[:size])
                store_slots(shape, "v", outs[1], start, slots, real[size:], imag[size:])

    result = vmem_call(
        "turn",
        body,
        [((4 * shape.rows, LANES), F32)] + [shape.array()] * (2 * size),
        inputs=(angles,) + sent_order(near) + sent_order(far) + (field_b[1], field_b[2]),
    )
    return result[0], result[1 : 1 + size], result[1 + size :]


def flip_raw(shape, own, other, hold=()):
    pieces = shape.rows // shape.part

    def body(own_ref, other_ref, out):
        total = jnp.zeros((TILE, LANES), F32)
        for start in range(0, shape.part, TILE):
            parts = [load_raw(own_ref, (i * shape.part + start) * 2) for i in range(pieces)]
            own_re, own_im = [p[0] for p in parts], [p[1] for p in parts]
            for i in range(pieces):
                other_re, other_im = load_raw(other_ref, (i * shape.part + start) * 2)
                total = total + other_re * flip_sum(own_im, i) - other_im * flip_sum(own_re, i)
        out[...] = sign(jnp.sum(total, axis=0, keepdims=True))

    return vmem_call("flip_raw", body, [((1, LANES), F32)], inputs=(own, other), hold=hold)[0]


def sign(value):
    return jnp.where(lax.axis_index("core") == 0, value, -value)


def flip_mats(low):
    small = flip_mat(LANES)
    zero = jnp.zeros_like(small)
    lane_flip = jnp.concatenate(
        [jnp.concatenate([small, zero], axis=1), jnp.concatenate([zero, small], axis=1)], axis=0
    )
    return lane_flip, flip_mat(low)


def gradients_mid(shape, field_b, own_before, other_before):
    low = shape.low

    def body(cost, cos_b, sin_b, own_ref, other_ref, out):
        lane_flip, row_flip = flip_mats(low)

        def turned(block, row):
            re, im = phased(
                block[:, :LANES], block[:, LANES:], cos_b[row : row + low, :], sin_b[row : row + low, :]
            )
            return jnp.concatenate([re, im], axis=1)

        near, far = (load_planes(shape, "all", [ref]) for ref in halves(shape, own_ref))
        other_far, other = (load_planes(shape, "other", [ref]) for ref in halves(shape, other_ref))
        inter = jnp.zeros((1, LANES), F32)
        mix_one = jnp.zeros((1, LANES), F32)
        mix_zero = jnp.zeros((1, LANES), F32)
        for u, flips in enumerate(flips_all(near, lane_flip, row_flip)):
            mix_one = mix_one + cross_imag(other[u], flips + 0.5 * far[u]) + cross_imag(other_far[u], 0.5 * near[u])
            weight = cost[u * low : (u + 1) * low, :]
            inter = inter + cross_imag(other[u], jnp.concatenate([weight] * 2, axis=1) * near[u])
        near = [turned(block, u * low) for u, block in enumerate(near)]
        for u, flips in enumerate(flips_all(near, lane_flip, row_flip)):
            across = 0.5 * turned(far[u], shape.rows + u * low)
            mix_zero = mix_zero + cross_imag(turned(other[u], u * low), flips + across)
            mix_zero = mix_zero + cross_imag(turned(other_far[u], shape.rows + u * low), 0.5 * near[u])
        out[...] = sign(jnp.concatenate([mix_zero, inter, mix_one], axis=0))

    return vmem_call(
        "gradients_mid", body, [((3, LANES), F32)], inputs=tuple(field_b) + (own_before, other_before)
    )[0]


def post_send(shape, angles, arrays, hold=()):
    count = len(arrays)

    def body(*refs):
        pair = angle_pair(refs[0], 1)
        for start in range(0, shape.part, TILE):
            for v in range(shape.depth):
                slots = [(u, v) for u in range(shape.depth)]
                real, imag = load_slots(shape, "u", plain_order(refs[1 : 1 + count]), start, slots)
                real, imag = butterflies(real, imag, pair, shape.bits("v"))
                store_slots(shape, "part", refs[1 + count :], start, slots, real, imag)

    size = ((2 * shape.rows * shape.batch // shape.depth, LANES), F32)
    return vmem_call(
        "post_send", body, [size] * (shape.depth // shape.batch), inputs=(angles,) + sent_order(arrays), hold=hold
    )


def flips_other(shape, other):
    def body(*refs):
        slots = shape.slots()
        for start in range(0, shape.part, TILE):
            real, imag = load_slots(shape, "other_part", refs[:-1], start, slots)
            flips = [[flip_sum(values, i) for i in range(len(slots))] for values in (real, imag)]
            store_slots(shape, "all", refs[-1:], start, slots, *flips)

    return vmem_call("flips_other", body, [shape.whole()], inputs=tuple(other))[0]


def post_mix(shape, angles, arrays, hold=()):
    count = len(arrays)

    def body(*refs):
        pair = angle_pair(refs[0], 1)
        for start in range(0, shape.part, TILE):
            for v in range(shape.depth):
                slots = [(u, v) for u in range(shape.depth)]
                real, imag = load_slots(shape, "u", plain_order(refs[1 : 1 + count]), start, slots)
                real, imag = butterflies(real, imag, pair, shape.bits("v"))
                store_slots(shape, "all", [refs[1 + count]], start, slots, real, imag)

    return vmem_call(
        "post_mix", body, [shape.whole()], inputs=(angles,) + sent_order(arrays), hold=hold
    )[0]


def post_grads(shape, mixed, other, flips, cost_a, hold=()):
    def body(mixed_ref, flips_ref, cost, *refs):
        others, out = refs[:-1], refs[-1]
        piece = shape.piece()
        slots = shape.slots()
        mix = jnp.zeros((TILE, LANES), F32)
        inter = jnp.zeros((TILE, LANES), F32)
        for start in range(0, shape.part, TILE):
            real, imag = load_slots(shape, "all", [mixed_ref], start, slots)
            other_re, other_im = load_slots(shape, "other_part", others, start, slots)
            flip_re, flip_im = load_slots(shape, "all", [flips_ref], start, slots)
            for i, slot in enumerate(slots):
                mix = mix + flip_re[i] * imag[i] - flip_im[i] * real[i]
                row = pl.multiple_of(piece(*slot) * shape.part + start, TILE)
                value = cost[pl.ds(row, TILE), :]
                inter = inter + value * (other_re[i] * imag[i] - other_im[i] * real[i])
        out[0:1, :] = sign(jnp.sum(inter, axis=0, keepdims=True))
        out[1:2, :] = sign(jnp.sum(mix, axis=0, keepdims=True))

    return vmem_call(
        "post_grads", body, [((2, LANES), F32)], inputs=(mixed, flips, cost_a, *other), hold=hold
    )[0]


def post_phase(shape, mixed, other, field_a):
    def body(own_ref, cos_a, sin_a, *refs):
        others, (psi_out, lam_out, token) = refs[:-3], refs[-3:]
        token[...] = jnp.zeros_like(token)
        first = lax.axis_index("core") == 0
        piece = shape.piece()
        slots = shape.slots()
        for start in range(0, shape.part, TILE):
            own_re, own_im = load_slots(shape, "all", [own_ref], start, slots)
            other_re, other_im = load_slots(shape, "other_part", others, start, slots)
            for i, slot in enumerate(slots):
                row = pl.multiple_of(piece(*slot) * shape.part + start, TILE)
                cosine, sine = cos_a[pl.ds(row, TILE), :], sin_a[pl.ds(row, TILE), :]
                own_pair = phased(own_re[i], own_im[i], cosine, sine)
                other_pair = phased(other_re[i], other_im[i], cosine, sine)
                for j in range(2):
                    span = pl.ds(2 * row + j, TILE, stride=2)
                    psi_out[span, :] = jnp.where(first, own_pair[j], other_pair[j])
                    lam_out[span, :] = jnp.where(first, other_pair[j], own_pair[j])

    return vmem_call(
        "post_phase",
        body,
        [shape.whole()] * 2 + [((TILE, LANES), F32)],
        inputs=(mixed, field_a[1], field_a[2], *other),
    )


AXES = ("grp", "z", "core")


def swap_cores(array):
    return lax.ppermute(array, "core", [(0, 1), (1, 0)])


def swap(shape, arrays, form):
    size = shape.depth
    out = list(arrays)
    with jax.named_scope("exchange_" + form):
        for i in sorted(range(1, size), key=lambda i: (i > 1, i.bit_count() == 1, -i)):
            pairs = []
            for chip in range(size * size):
                for core in range(CORES):
                    step = i if (core == 0) == (form == "u") else i * size
                    pairs.append((chip * CORES + core, (chip ^ step) * CORES + core))
            out[i] = lax.ppermute(arrays[i], AXES, pairs)
    return out


def total_grads(shape, parts, token=None):
    def join(early, mid_part, late, out):
        rows = [late[0:1, :], late[1:2, :] + mid_part[0:1, :], mid_part[1:2, :], mid_part[2:3, :] + early[...]]
        out[...] = jnp.concatenate(rows + [jnp.zeros((TILE - 4, LANES), F32)], axis=0)

    def add(*refs):
        values = [ref[...] for ref in refs[:-1]]
        while len(values) > 1:
            values = [left + right for left, right in zip(values[::2], values[1::2])]
        refs[-1][...] = values[0]

    block_shape = [((TILE, LANES), F32)]
    block = vmem_call("join_grads", join, block_shape, inputs=tuple(parts))[0]
    for axis, size, most in (("core", CORES, 2), ("grp", shape.groups, 4), ("z", shape.depth, 4)):
        stride = 1
        while stride < size:
            reach = min(most, size // stride)
            others = [
                lax.ppermute(block, axis, [(j, j ^ (stride * i)) for j in range(size)]) for i in range(1, reach)
            ]
            last = axis == "z" and stride * reach == size and token is not None
            hold = (token,) if last else ()
            block = vmem_call("add_grads", add, block_shape, inputs=(block, *others), hold=hold)[0]
            stride *= reach
    scale = 2.0 / (shape.rows * LANES * shape.devices)

    def finish(ref, out):
        summed = jnp.sum(ref[...], axis=1, keepdims=True) * scale
        for i in range(2 * LAYERS):
            out[i] = jnp.sum(summed[i : i + 1, :])

    return vmem_call("finish_grads", finish, [((2 * LAYERS,), F32)], inputs=(block,), smem_out=True)[0]


def after(values, first):
    return lax.optimization_barrier((values, first))[0]


def piece_mix(shape, angles, which, state):
    low = shape.low
    least = shape.part.bit_length() - 1

    def body(angle, ref, mixed, flipped):
        sine, cosine = half_angle(angle[0:1, which : which + 1])
        real, imag = mixer_mats(low, cosine, sine, least)
        row_high, row_low = split(jnp.concatenate([real, imag], axis=0))
        row_flip = flip_mat(low, least)
        blocks = [ref[i * low : (i + 1) * low, :] for i in range(shape.planes)]
        for i, (re, im) in enumerate(rotate_all(blocks, None, None, row_high, row_low, cosine, sine)):
            mixed[i * low : (i + 1) * low, :LANES] = re
            mixed[i * low : (i + 1) * low, LANES:] = im
        for i, block in enumerate(flips_all(blocks, None, row_flip)):
            flipped[i * low : (i + 1) * low, :] = block

    return vmem_call(
        "piece_mix",
        body, [((shape.rows, 2 * LANES), F32)] * 2, inputs=(angles, state,)
    )


def plain_cross(lam, other):
    def body(lam_ref, other_ref, out):
        out[...] = cross_imag(lam_ref[...], other_ref[...])

    return vmem_call("plain_cross", body, [((1, LANES), F32)], inputs=(lam, other))[0]


def plain_gradients(shape, field_b, psi_before, lam_before):
    low = shape.low

    def body(cost, cos_b, sin_b, psi_ref, lam_ref, out):
        lane_flip, row_flip = flip_mats(low)
        spans = [slice(i * low, (i + 1) * low) for i in range(shape.planes)]
        psi = [psi_ref[span, :] for span in spans]
        lam = [lam_ref[span, :] for span in spans]
        inter = jnp.zeros((1, LANES), F32)
        mix_one = jnp.zeros((1, LANES), F32)
        mix_zero = jnp.zeros((1, LANES), F32)
        for i, flips in enumerate(flips_all(psi, lane_flip, row_flip)):
            mix_one = mix_one + cross_imag(lam[i], flips)
            inter = inter + cross_imag(lam[i], jnp.concatenate([cost[spans[i], :]] * 2, axis=1) * psi[i])

        def turned(block, span):
            re, im = phased(block[:, :LANES], block[:, LANES:], cos_b[span, :], sin_b[span, :])
            return jnp.concatenate([re, im], axis=1)

        psi = [turned(block, span) for block, span in zip(psi, spans)]
        for i, flips in enumerate(flips_all(psi, lane_flip, row_flip)):
            mix_zero = mix_zero + cross_imag(turned(lam[i], spans[i]), flips)
        out[...] = jnp.concatenate([mix_zero, inter, mix_one], axis=0)

    return vmem_call("plain_gradients", body, [((3, LANES), F32)], inputs=tuple(field_b) + (psi_before, lam_before))[0]


def plain_phase(shape, state, field, gradient):
    def body(ref, cost, cosine, sine, out):
        real, imag = ref[:, :LANES], ref[:, LANES:]
        if gradient:
            re, im = cost[...] * real, cost[...] * imag
        else:
            re, im = phased(real, imag, cosine[...], sine[...])
        out[:, :LANES] = re
        out[:, LANES:] = im

    return vmem_call("plain_phase", body, [((shape.rows, 2 * LANES), F32)], inputs=(state,) + tuple(field))[0]


def mid_math(shape, angles, planes, mats, cos_b, sin_b):
    low = shape.low
    sine, cosine = half_angle(angles[0:1, 3:4])
    first = rotate_all(planes, *[m[...] for m in mats[4:8]], cosine, sine)
    turned = []
    for i, (re, im) in enumerate(first):
        re, im = phased(re, im, cos_b[i * low : (i + 1) * low, :], sin_b[i * low : (i + 1) * low, :])
        turned.append(jnp.concatenate([re, im], axis=1))
    sine, cosine = half_angle(angles[0:1, 1:2])
    second = rotate_all(turned, *[m[...] for m in mats[0:4]], cosine, sine)
    return first, second


def plain_mid(shape, angles, state, field_b, mats):
    low = shape.low

    def body(angle, ref, cos_b, sin_b, *rest):
        blocks = [ref[i * low : (i + 1) * low, :] for i in range(shape.planes)]
        for out, pairs in zip(rest[8:], mid_math(shape, angle, blocks, rest[:8], cos_b, sin_b)):
            for i, (re, im) in enumerate(pairs):
                out[i * low : (i + 1) * low, :LANES] = re
                out[i * low : (i + 1) * low, LANES:] = im

    return vmem_call(
        "plain_mid",
        body,
        [((shape.rows, 2 * LANES), F32)] * 2,
        inputs=(angles, state, field_b[1], field_b[2]) + tuple(mats[0]) + tuple(mats[1]),
    )


def exchange_all(shape, state):
    block = state.reshape(shape.devices, -1, 2 * LANES)
    return lax.all_to_all(block, AXES, 0, 0, tiled=True).reshape(state.shape)


def plain(shape, forward, adjoint, edges, weights, layout, slab_bits, angles):
    rows = shape.rows

    def wide(array):
        return array.reshape(2, rows, LANES).transpose(1, 0, 2).reshape(rows, 2 * LANES)

    def narrow(array):
        return array.reshape(rows, 2, LANES).transpose(1, 0, 2).reshape(2, rows * LANES)

    def before(row):
        return shape.own() * rows + row

    def beyond(row):
        return (row // shape.part) * rows + shape.own() * shape.part + row % shape.part

    angles = angles.reshape(1, -1)
    small = small_inputs(edges, weights, layout, slab_bits)
    fields = make_fields(angles, *small, (rows, rows), before, beyond, shape.known)
    field_a, field_b = fields[:3], fields[3:]
    mats = make_mats(angles, shape.low)
    psi, flips = piece_mix(shape, angles, 3, wide(forward))
    lam, _ = piece_mix(shape, angles, 3, wide(adjoint))
    early = plain_cross(wide(adjoint), flips)
    psi_before, psi_after = plain_mid(shape, angles, exchange_all(shape, psi), field_b, mats)
    lam_before, lam_after = plain_mid(shape, angles, exchange_all(shape, lam), field_b, mats)
    mid_part = plain_gradients(shape, field_b, psi_before, lam_before)
    psi, lam = exchange_all(shape, psi_after), exchange_all(shape, lam_after)
    psi_mixed, flips = piece_mix(shape, angles, 1, psi)
    lam_mixed, _ = piece_mix(shape, angles, 1, lam)
    late = jnp.concatenate(
        [plain_cross(lam_mixed, plain_phase(shape, psi_mixed, field_a, True)), plain_cross(lam, flips)], axis=0
    )
    grads = total_grads(shape, (early, mid_part, late))
    outs = [narrow(plain_phase(shape, state, field_a, False)) for state in (psi_mixed, lam_mixed)]
    return outs[0], outs[1], grads


def interleave(array, rows):
    return array.reshape(2, rows, LANES).transpose(1, 0, 2).reshape(2 * rows, LANES)


def deinterleave(array, rows):
    return array.reshape(rows, 2, LANES).transpose(1, 0, 2).reshape(2, rows * LANES)


def places(shape):
    def before(row):
        return shape.own() * shape.rows + row

    def beyond(row):
        far, slot, inner = row // shape.rows, (row % shape.rows) // shape.part, row % shape.part
        source = shape.piece()(slot // shape.depth, slot % shape.depth) * CORES
        source = source + jnp.bitwise_xor(lax.axis_index("core"), far)
        return source * shape.rows + shape.chip() * shape.part + inner

    return before, beyond


def pipelined(shape, forward, adjoint, edges, weights, layout, slab_bits, angles):
    rows = shape.rows
    angles = angles.reshape(1, -1)
    own_raw, other_raw, near = pre_near(shape, angles, interleave(forward, rows), interleave(adjoint, rows))
    far_raw = swap_cores(other_raw)
    mats = make_mats(angles, shape.low, hold=near[:1])
    before, beyond = places(shape)
    small = small_inputs(edges, weights, layout, slab_bits)
    sizes = (rows, 2 * rows), before, beyond, shape.known
    fields = make_fields(angles, *small, *sizes, core=1, hold=near[:1])
    near = swap(shape, near, "u")
    far = swap(shape, pre_far(shape, angles, far_raw), "u")
    near = swap(shape, rotate_local(shape, angles, near, "u", "v", mats[1], 3, hold=fields[:1]), "v")
    far = rotate_local(shape, angles, far, "u", "v", mats[1], 3)
    fields = make_fields(angles, *small, *sizes, core=0, hold=after(fields, far[0]))
    field_a, field_b = fields[:3], fields[3:]
    early = flip_raw(shape, own_raw, other_raw, hold=far[:1])
    far = swap(shape, far, "v")
    own_before, near, far = turn(shape, angles, near, far, field_b)
    far = swap(shape, far, "v")
    near = swap(shape, near, "v")
    other_before = swap_cores(own_before)
    far = swap(shape, rotate_local(shape, angles, far, "v", "u", mats[0], 1, hold=(other_before,)), "u")
    near = rotate_local(shape, angles, near, "v", "u", mats[0], 1)
    mid_part = gradients_mid(shape, field_b, own_before, other_before)
    other = [swap_cores(array) for array in post_send(shape, angles, far, hold=(near[0], mid_part, early))]
    near = swap(shape, near, "u")
    flips = flips_other(shape, other)
    mixed = post_mix(shape, angles, near, hold=(mid_part, early))
    late = post_grads(shape, mixed, other, flips, field_a[0])
    psi_out, lam_out, token = post_phase(shape, mixed, other, field_a)
    grads = total_grads(shape, (early, mid_part, late), token)
    return deinterleave(psi_out, rows), deinterleave(lam_out, rows), grads


def solution(mesh):
    groups, rest = mesh.shape["grp"], mesh.shape["rep"]
    depth = rest // CORES
    fine = Mesh(mesh.devices.reshape(groups, depth, CORES), AXES)

    def per_device(forward, *others):
        shape = Shape(groups, depth, forward.shape[1])
        return (pipelined if shape.tiles else plain)(shape, forward, *others)

    state = P(None, AXES)
    return jax.shard_map(
        per_device,
        mesh=fine,
        in_specs=(state, state, P(), P(), P(), P(), P()),
        out_specs=(state, state, P()),
        check_vma=False,
    )
```

```python
import jax
import jax.numpy as jnp
from jax import lax
from jax.experimental import pallas as pl
from jax.experimental.pallas import tpu as pltpu
from jax.sharding import Mesh, PartitionSpec as P

NODES = 40
LAYERS = 2
LANES = 128
TILE = 8
CORES = 2
F32 = jnp.float32
BF16 = jnp.bfloat16
VMEM_LIMIT = 12 << 20
PIECES = 4
VMEM_FIRST = 52 << 20


def vmem_call(name, body, out_shapes, inputs=(), smem_out=False, hold=()):
    if hold:
        taken = len(inputs)
        inner = body

        def body(*refs):
            inner(*refs[:taken], *refs[taken + len(hold) :])

        inputs = tuple(inputs) + tuple(hold)
    specs = [pl.BlockSpec(memory_space=pltpu.VMEM)] * len(inputs)
    place = pltpu.SMEM if smem_out else pltpu.VMEM
    return pl.pallas_call(
        body,
        name=name,
        out_shape=[jax.ShapeDtypeStruct(shape, kind) for shape, kind in out_shapes],
        in_specs=specs,
        out_specs=[pl.BlockSpec(memory_space=place)] * len(out_shapes),
        compiler_params=pltpu.CompilerParams(vmem_limit_bytes=VMEM_LIMIT),
    )(*inputs)


def half_angle(x):
    y = 0.5 * x
    z = y * y
    sin_y = jnp.full_like(z, -1.0 / 1307674368000.0)
    for factor in (6227020800.0, -39916800.0, 362880.0, -5040.0, 120.0, -6.0, 1.0):
        sin_y = sin_y * z + 1.0 / factor
    sin_y = sin_y * y
    cos_y = jnp.full_like(z, 1.0 / 20922789888000.0)
    for factor in (-87178291200.0, 479001600.0, -3628800.0, 40320.0, -720.0, 24.0, -2.0, 1.0):
        cos_y = cos_y * z + 1.0 / factor
    return 2.0 * sin_y * cos_y, 1.0 - 2.0 * sin_y * sin_y


def split(value):
    high = value.astype(BF16)
    return high, (value - high.astype(F32)).astype(BF16)


def dot(left, right):
    return jnp.dot(left, right, preferred_element_type=F32)


def mixer_mats(size, cos_beta, sin_beta, least=0):
    row = lax.broadcasted_iota(jnp.int32, (size, size), 0)
    col = lax.broadcasted_iota(jnp.int32, (size, size), 1)
    differ = jnp.bitwise_xor(row, col)
    real = jnp.ones((size, size), F32)
    real = jnp.where(jnp.bitwise_and(differ, (1 << least) - 1) == 0, real, 0.0)
    imag = jnp.zeros((size, size), F32)
    for bit in range(least, size.bit_length() - 1):
        flagged = jnp.bitwise_and(differ, 1 << bit) != 0
        real, imag = (
            jnp.where(flagged, -imag * sin_beta, real * cos_beta),
            jnp.where(flagged, real * sin_beta, imag * cos_beta),
        )
    return real, imag


def flip_mat(size, least=0):
    row = lax.broadcasted_iota(jnp.int32, (size, size), 0)
    col = lax.broadcasted_iota(jnp.int32, (size, size), 1)
    differ = jnp.bitwise_xor(row, col)
    count = jnp.zeros((size, size), jnp.int32)
    for bit in range(size.bit_length() - 1):
        count = count + jnp.bitwise_and(differ >> bit, 1)
    rest = jnp.bitwise_and(differ, (1 << least) - 1)
    return jnp.where(jnp.logical_and(count == 1, rest == 0), 1.0, 0.0).astype(BF16)


def rotate_all(planes, lane_high, lane_low, row_high, row_low, cos_beta, sin_beta):
    low = planes[0].shape[0]
    mixed = []
    for block in planes:
        high, rest = split(block)
        if lane_high is not None:
            lanes = dot(high, lane_high) + dot(rest, lane_high) + dot(high, lane_low)
            high, rest = split(lanes)
        both = dot(row_high, high) + dot(row_high, rest) + dot(row_low, high)
        real = both[:low, :LANES] - both[low:, LANES:]
        imag = both[:low, LANES:] + both[low:, :LANES]
        mixed.append((real, imag))
    stride = 1
    while stride < len(mixed):
        for first in range(len(mixed)):
            if first & stride:
                continue
            (ar, ai), (br, bi) = mixed[first], mixed[first + stride]
            mixed[first] = (cos_beta * ar - sin_beta * bi, cos_beta * ai + sin_beta * br)
            mixed[first + stride] = (cos_beta * br - sin_beta * ai, cos_beta * bi + sin_beta * ar)
        stride *= 2
    return mixed


def flips_all(planes, lane_flip, row_flip):
    out = []
    for index, block in enumerate(planes):
        high, rest = split(block)
        total = dot(row_flip, high) + dot(row_flip, rest)
        if lane_flip is not None:
            total = total + dot(high, lane_flip) + dot(rest, lane_flip)
        stride = 1
        while stride < len(planes):
            total = total + planes[index ^ stride]
            stride *= 2
        out.append(total)
    return out


def fold_rows(value):
    folded = value[:TILE]
    for start in range(TILE, value.shape[0], TILE):
        folded = folded + value[start : start + TILE]
    return jnp.sum(folded, axis=0, keepdims=True)


def cross_imag(lam, other):
    return fold_rows(lam[:, :LANES] * other[:, LANES:] - lam[:, LANES:] * other[:, :LANES])


def spin_rows(position, layout, slab, known):
    lane_bits = LANES.bit_length() - 1
    shift = jnp.clip(layout - lane_bits, 0, known - 1)
    inside = jnp.bitwise_and(jnp.right_shift(position, shift), 1)
    bit = jnp.where(layout < known + lane_bits, inside, slab)
    return jnp.where(layout < lane_bits, 0, 1 - 2 * bit).astype(F32)


def field_body(place_first, place_second, known):
    lane_bits = LANES.bit_length() - 1

    def body(angles, edges, weights, layout, slab, cost_a, cos_a, sin_a, cost_b, cos_b, sin_b):
        node = lax.broadcasted_iota(jnp.int32, (NODES, edges.shape[1]), 0)
        first = jnp.where(edges[0:1, :] == node, 1.0, 0.0)
        second = jnp.where(edges[1:2, :] == node, 1.0, 0.0)
        weight = weights[...].astype(F32)
        total = jnp.sum(weight, axis=1, keepdims=True)
        exact = lax.Precision.HIGHEST

        def full(left, right, dims):
            return lax.dot_general(left, right, dims, precision=exact, preferred_element_type=F32)

        plain = (((1,), (0,)), ((), ()))
        turned = (((1,), (1,)), ((), ()))
        matrix = full(first * weight, second, turned) + full(second * weight, first, turned)
        lane = lax.broadcasted_iota(jnp.int32, (LANES, NODES), 0)
        lane_layout = layout[...]
        lane_bit = jnp.bitwise_and(jnp.right_shift(lane, jnp.clip(lane_layout, 0, lane_bits - 1)), 1)
        lane_spin = jnp.where(lane_layout < lane_bits, 1 - 2 * lane_bit, 0).astype(F32)
        lane_energy = full(jnp.ones((TILE, NODES), F32), lane_spin * full(lane_spin, matrix, plain), turned)[0:1]

        def field(position, cost, cos_out, sin_out, gamma):
            spins = spin_rows(position, lane_layout, slab[...], known)
            pulled = full(spins, matrix, plain)
            energy = jnp.sum(pulled * spins, axis=1, keepdims=True)
            energy = energy + lane_energy + 2.0 * full(pulled, lane_spin, turned)
            value = 2.0 - energy / total
            cost[...] = value
            sine, cosine = half_angle(gamma * value)
            cos_out[...] = cosine
            sin_out[...] = sine

        row = lax.broadcasted_iota(jnp.int32, (cost_a.shape[0], 1), 0)
        field(place_first(row), cost_a, cos_a, sin_a, angles[0:1, 0:1])
        row = lax.broadcasted_iota(jnp.int32, (cost_b.shape[0], 1), 0)
        field(place_second(row), cost_b, cos_b, sin_b, angles[0:1, 2:3])
    return body


def make_fields(angles, edges, weights, layout, slab, rows, place_first, place_second, known, core=None, hold=()):
    inner = field_body(place_first, place_second, known)
    shapes = [((rows[0], LANES), F32)] * 3 + [((rows[1], LANES), F32)] * 3
    small = (angles, edges, weights, layout, slab)
    held = tuple(hold)

    def body(*refs):
        refs = refs[: len(small)] + refs[len(small) + len(held) :]
        if core is None:
            inner(*refs)
        else:

            @pl.when(lax.axis_index("core") == core)
            def _():
                inner(*refs)

    return pl.pallas_call(
        body,
        name="make_fields",
        out_shape=[jax.ShapeDtypeStruct(size, kind) for size, kind in shapes],
        in_specs=[pl.BlockSpec(memory_space=pltpu.VMEM)] * (len(small) + len(held)),
        out_specs=[pl.BlockSpec(memory_space=pltpu.VMEM)] * len(shapes),
        input_output_aliases={len(small) + i: i for i in range(len(shapes))} if len(held) == len(shapes) else {},
        compiler_params=pltpu.CompilerParams(vmem_limit_bytes=VMEM_LIMIT),
    )(*small, *held)


def make_mats(angles, low, hold=()):
    def body(angles, *mats):
        for layer in range(LAYERS):
            sine, cosine = half_angle(angles[0:1, 2 * layer + 1 : 2 * layer + 2])
            real, imag = mixer_mats(LANES, cosine, sine)
            lanes = jnp.concatenate(
                [jnp.concatenate([real, imag], axis=1), jnp.concatenate([-imag, real], axis=1)], axis=0
            )
            mats[4 * layer][...], mats[4 * layer + 1][...] = split(lanes)
            real, imag = mixer_mats(low, cosine, sine)
            mats[4 * layer + 2][...], mats[4 * layer + 3][...] = split(jnp.concatenate([real, imag], axis=0))

    shapes = ([((2 * LANES, 2 * LANES), BF16)] * 2 + [((2 * low, low), BF16)] * 2) * LAYERS
    out = vmem_call("make_mats", body, shapes, inputs=(angles,), hold=hold)
    return [out[4 * layer : 4 + 4 * layer] for layer in range(LAYERS)]


def small_inputs(edges, weights, layout, slab_bits):
    return edges.T, weights.reshape(1, -1), layout.reshape(1, -1), slab_bits.reshape(1, -1)


class Shape:
    def __init__(self, groups, depth, amp_dev):
        self.groups = groups
        self.depth = depth
        self.devices = groups * depth * CORES
        self.rows = amp_dev // LANES
        self.known = (self.rows * self.devices).bit_length() - 1
        self.tiles = groups == depth and self.rows % (groups * depth * TILE) == 0
        self.part = self.rows // (groups * depth if self.tiles else self.devices)
        self.low = depth * self.part if self.tiles else min(self.rows, 2 * LANES)
        self.planes = self.rows // self.low
        self.batch = max(depth // PIECES, 1)

    def own(self):
        return self.chip() * CORES + lax.axis_index("core")

    def chip(self):
        return lax.axis_index("grp") * self.depth + lax.axis_index("z")

    def slots(self):
        return [(u, v) for u in range(self.depth) for v in range(self.depth)]

    def bits(self, letters):
        each = self.depth.bit_length() - 1
        return [bit + (each if letter == "u" else 0) for letter in letters for bit in range(each)]

    def piece(self):
        core = lax.axis_index("core")
        chip = self.chip()
        step_u = 1 + core * (self.depth - 1)
        step_v = self.depth - core * (self.depth - 1)
        return lambda u, v: jnp.bitwise_xor(chip, u * step_u + v * step_v)

    def array(self):
        return ((2 * self.rows // self.depth, LANES), F32)

    def whole(self):
        return ((2 * self.rows, LANES), F32)

    def place(self, form, refs, u, v):
        index, inner = {
            "u": (u, v),
            "v": (v, u),
            "all": (0, u * self.depth + v),
            "other": (0, v * self.depth + u),
            "part": (u // self.batch, u % self.batch * self.depth + v),
            "other_part": (v // self.batch, v % self.batch * self.depth + u),
        }[form]
        return refs[index], inner * 2 * self.part


def angle_pair(angles, which):
    return half_angle(jnp.broadcast_to(angles[0:1, which : which + 1], (TILE, LANES)))


def butterflies(real, imag, pair, bits):
    sine, cosine = pair
    tangent = sine / cosine
    scale = cosine
    for _ in bits[1:]:
        scale = scale * cosine
    for bit in bits:
        for first in range(len(real)):
            other = first | (1 << bit)
            if other == first:
                continue
            ar, ai, br, bi = real[first], imag[first], real[other], imag[other]
            real[first], imag[first] = ar - tangent * bi, ai + tangent * br
            real[other], imag[other] = br - tangent * ai, bi + tangent * ar
    return [scale * v for v in real], [scale * v for v in imag]


def flip_sum(values, index):
    total = None
    stride = 1
    while stride < len(values):
        term = values[index ^ stride]
        total = term if total is None else total + term
        stride *= 2
    return total


def sent_order(arrays):
    return tuple(arrays[2:]) + (arrays[1], arrays[0])


def plain_order(arrays):
    return (arrays[-1], arrays[-2]) + tuple(arrays[:-2])


def load_slots(shape, form, refs, start, slots):
    real, imag = [], []
    for slot in slots:
        ref, base = shape.place(form, refs, *slot)
        real.append(ref[base + start : base + start + TILE, :])
        imag.append(ref[base + shape.part + start : base + shape.part + start + TILE, :])
    return real, imag


def store_slots(shape, form, refs, start, slots, real, imag):
    for slot, re, im in zip(slots, real, imag):
        ref, base = shape.place(form, refs, *slot)
        ref[base + start : base + start + TILE, :] = re
        ref[base + shape.part + start : base + shape.part + start + TILE, :] = im


def load_planes(shape, form, refs):
    planes = []
    for u in range(shape.depth):
        pairs = []
        for v in range(shape.depth):
            ref, base = shape.place(form, refs, u, v)
            middle = base + shape.part
            pairs.append(jnp.concatenate([ref[base:middle, :], ref[middle : middle + shape.part, :]], axis=1))
        planes.append(jnp.concatenate(pairs, axis=0))
    return planes


def store_planes(shape, form, refs, planes):
    for u, v in shape.slots():
        re, im = planes[u]
        at = v * shape.part
        ref, base = shape.place(form, refs, u, v)
        middle = base + shape.part
        ref[base:middle, :] = re[at : at + shape.part]
        ref[middle : middle + shape.part, :] = im[at : at + shape.part]


def phased(real, imag, cosine, sine):
    return real * cosine - imag * sine, imag * cosine + real * sine


def load_raw(ref, base):
    return ref[pl.ds(base, TILE, stride=2), :], ref[pl.ds(base + 1, TILE, stride=2), :]


def first_rotations(shape, angle, raw, outs):
    piece = shape.piece()
    pair = angle_pair(angle, 3)
    for start in range(0, shape.part, TILE):
        for v in range(shape.depth):
            slots = [(u, v) for u in range(shape.depth)]
            parts = [load_raw(raw, (piece(*slot) * shape.part + start) * 2) for slot in slots]
            real, imag = butterflies([p[0] for p in parts], [p[1] for p in parts], pair, shape.bits("v"))
            store_slots(shape, "u", outs, start, slots, real, imag)


COPIES = 4


def pre_near(shape, angles, psi, lam):
    step = 2 * shape.rows // COPIES

    def body(angle, psi_ref, lam_ref, own, send, *rest):
        outs, angle_here, sems = rest[:-2], rest[-2], rest[-1]
        fetch = pltpu.make_async_copy(angle, angle_here, sems.at[2 * COPIES])
        fetch.start()

        def copies(own_ref, send_ref):
            pairs = [(own_ref, own, 0), (send_ref, send, COPIES)]
            return [
                pltpu.make_async_copy(
                    source.at[pl.ds(i * step, step), :], target.at[pl.ds(i * step, step), :], sems.at[first + i]
                )
                for source, target, first in pairs
                for i in range(COPIES)
            ]

        @pl.when(lax.axis_index("core") == 0)
        def _():
            for copy in copies(psi_ref, lam_ref):
                copy.start()

        @pl.when(lax.axis_index("core") != 0)
        def _():
            for copy in copies(lam_ref, psi_ref):
                copy.start()

        waits = copies(psi_ref, lam_ref)
        fetch.wait()
        for copy in waits[:COPIES]:
            copy.wait()
        first_rotations(shape, angle_here, own, outs)
        for copy in waits[COPIES:]:
            copy.wait()

    shapes = [shape.whole()] * 2 + [shape.array()] * shape.depth
    out = pl.pallas_call(
        body,
        name="pre_near",
        out_shape=[jax.ShapeDtypeStruct(size, kind) for size, kind in shapes],
        in_specs=[pl.BlockSpec(memory_space=pltpu.HBM)] * 3,
        out_specs=[pl.BlockSpec(memory_space=pltpu.VMEM)] * len(shapes),
        scratch_shapes=[pltpu.VMEM(angles.shape, F32), pltpu.SemaphoreType.DMA((2 * COPIES + 1,))],
        compiler_params=pltpu.CompilerParams(vmem_limit_bytes=VMEM_FIRST),
    )(angles, psi, lam)
    return out[0], out[1], out[2:]


def pre_far(shape, angles, raw):
    def body(angle, ref, *outs):
        first_rotations(shape, angle, ref, outs)

    return vmem_call("pre_far", body, [shape.array()] * shape.depth, inputs=(angles, raw))


def rotate_local(shape, angles, arrays, form, new_form, mats, which, hold=()):
    count = len(arrays)

    def body(*refs):
        matrices = [m[...] for m in refs[1 + count : 5 + count]]
        sine, cosine = half_angle(refs[0][0:1, which : which + 1])
        planes = load_planes(shape, form, plain_order(refs[1 : 1 + count]))
        store_planes(shape, new_form, refs[5 + count :], rotate_all(planes, *matrices, cosine, sine))

    return vmem_call(
        "rotate_local",
        body,
        [shape.array()] * shape.depth,
        inputs=(angles,) + sent_order(arrays) + tuple(mats),
        hold=hold,
    )


def halves(shape, ref):
    size = 2 * shape.rows
    return [ref.at[pl.ds(i * size, size), :] for i in range(2)]


def turn(shape, angles, near, far, field_b):
    size = shape.depth

    def body(*refs):
        states = plain_order(refs[1 : 1 + size]), plain_order(refs[1 + size : 1 + 2 * size])
        cos_b, sin_b = refs[1 + 2 * size : 3 + 2 * size]
        before = halves(shape, refs[3 + 2 * size])
        outs = refs[4 + 2 * size : 4 + 3 * size], refs[4 + 3 * size :]
        pair_one, pair_zero = angle_pair(refs[0], 3), angle_pair(refs[0], 1)
        bits = list(range(size.bit_length()))
        for start in range(0, shape.part, TILE):
            for u in range(size):
                slots = [(u, v) for v in range(size)]
                real, imag = load_slots(shape, "v", states[0], start, slots)
                far_real, far_imag = load_slots(shape, "v", states[1], start, slots)
                real, imag = butterflies(real + far_real, imag + far_imag, pair_one, bits)
                store_slots(shape, "all", before[:1], start, slots, real[:size], imag[:size])
                store_slots(shape, "all", before[1:], start, slots, real[size:], imag[size:])
                for i in range(2 * size):
                    row = (i // size) * shape.rows + (u * size + i % size) * shape.part + start
                    real[i], imag[i] = phased(
                        real[i], imag[i], cos_b[row : row + TILE, :], sin_b[row : row + TILE, :]
                    )
                real, imag = butterflies(real, imag, pair_zero, bits)
                store_slots(shape, "v", outs[0], start, slots, real[:size], imag[:size])
                store_slots(shape, "v", outs[1], start, slots, real[size:], imag[size:])

    result = vmem_call(
        "turn",
        body,
        [((4 * shape.rows, LANES), F32)] + [shape.array()] * (2 * size),
        inputs=(angles,) + sent_order(near) + sent_order(far) + (field_b[1], field_b[2]),
    )
    return result[0], result[1 : 1 + size], result[1 + size :]


def flip_raw(shape, own, other, hold=()):
    pieces = shape.rows // shape.part

    def body(own_ref, other_ref, out):
        total = jnp.zeros((TILE, LANES), F32)
        for start in range(0, shape.part, TILE):
            parts = [load_raw(own_ref, (i * shape.part + start) * 2) for i in range(pieces)]
            own_re, own_im = [p[0] for p in parts], [p[1] for p in parts]
            for i in range(pieces):
                other_re, other_im = load_raw(other_ref, (i * shape.part + start) * 2)
                total = total + other_re * flip_sum(own_im, i) - other_im * flip_sum(own_re, i)
        out[...] = sign(jnp.sum(total, axis=0, keepdims=True))

    return vmem_call("flip_raw", body, [((1, LANES), F32)], inputs=(own, other), hold=hold)[0]


def sign(value):
    return jnp.where(lax.axis_index("core") == 0, value, -value)


def flip_mats(low):
    small = flip_mat(LANES)
    zero = jnp.zeros_like(small)
    lane_flip = jnp.concatenate(
        [jnp.concatenate([small, zero], axis=1), jnp.concatenate([zero, small], axis=1)], axis=0
    )
    return lane_flip, flip_mat(low)


def gradients_mid(shape, field_b, own_before, other_before):
    low = shape.low

    def body(cost, cos_b, sin_b, own_ref, other_ref, out):
        lane_flip, row_flip = flip_mats(low)

        def turned(block, row):
            re, im = phased(
                block[:, :LANES], block[:, LANES:], cos_b[row : row + low, :], sin_b[row : row + low, :]
            )
            return jnp.concatenate([re, im], axis=1)

        near, far = (load_planes(shape, "all", [ref]) for ref in halves(shape, own_ref))
        other_far, other = (load_planes(shape, "other", [ref]) for ref in halves(shape, other_ref))
        inter = jnp.zeros((1, LANES), F32)
        mix_one = jnp.zeros((1, LANES), F32)
        mix_zero = jnp.zeros((1, LANES), F32)
        for u, flips in enumerate(flips_all(near, lane_flip, row_flip)):
            mix_one = mix_one + cross_imag(other[u], flips + 0.5 * far[u]) + cross_imag(other_far[u], 0.5 * near[u])
            weight = cost[u * low : (u + 1) * low, :]
            inter = inter + cross_imag(other[u], jnp.concatenate([weight] * 2, axis=1) * near[u])
        near = [turned(block, u * low) for u, block in enumerate(near)]
        for u, flips in enumerate(flips_all(near, lane_flip, row_flip)):
            across = 0.5 * turned(far[u], shape.rows + u * low)
            mix_zero = mix_zero + cross_imag(turned(other[u], u * low), flips + across)
            mix_zero = mix_zero + cross_imag(turned(other_far[u], shape.rows + u * low), 0.5 * near[u])
        out[...] = sign(jnp.concatenate([mix_zero, inter, mix_one], axis=0))

    return vmem_call(
        "gradients_mid", body, [((3, LANES), F32)], inputs=tuple(field_b) + (own_before, other_before)
    )[0]


def post_send(shape, angles, arrays, hold=()):
    count = len(arrays)

    def body(*refs):
        pair = angle_pair(refs[0], 1)
        for start in range(0, shape.part, TILE):
            for v in range(shape.depth):
                slots = [(u, v) for u in range(shape.depth)]
                real, imag = load_slots(shape, "u", plain_order(refs[1 : 1 + count]), start, slots)
                real, imag = butterflies(real, imag, pair, shape.bits("v"))
                store_slots(shape, "part", refs[1 + count :], start, slots, real, imag)

    size = ((2 * shape.rows * shape.batch // shape.depth, LANES), F32)
    return vmem_call(
        "post_send", body, [size] * (shape.depth // shape.batch), inputs=(angles,) + sent_order(arrays), hold=hold
    )


def post_mix(shape, angles, arrays, hold=()):
    count = len(arrays)

    def body(*refs):
        pair = angle_pair(refs[0], 1)
        for start in range(0, shape.part, TILE):
            for v in range(shape.depth):
                slots = [(u, v) for u in range(shape.depth)]
                real, imag = load_slots(shape, "u", plain_order(refs[1 : 1 + count]), start, slots)
                real, imag = butterflies(real, imag, pair, shape.bits("v"))
                store_slots(shape, "all", [refs[1 + count]], start, slots, real, imag)

    return vmem_call(
        "post_mix", body, [shape.whole()], inputs=(angles,) + sent_order(arrays), hold=hold
    )[0]


def post_grads(shape, mixed, other, cost_a, early, mid_part):
    def body(mixed_ref, cost, early_ref, mid_ref, *refs):
        others, out = refs[:-1], refs[-1]
        piece = shape.piece()
        slots = shape.slots()
        mix = jnp.zeros((TILE, LANES), F32)
        inter = jnp.zeros((TILE, LANES), F32)
        for start in range(0, shape.part, TILE):
            real, imag = load_slots(shape, "all", [mixed_ref], start, slots)
            other_re, other_im = load_slots(shape, "other_part", others, start, slots)
            for i, slot in enumerate(slots):
                mix = mix + flip_sum(other_re, i) * imag[i] - flip_sum(other_im, i) * real[i]
                row = pl.multiple_of(piece(*slot) * shape.part + start, TILE)
                value = cost[pl.ds(row, TILE), :]
                inter = inter + value * (other_re[i] * imag[i] - other_im[i] * real[i])
        rows = [
            sign(jnp.sum(inter, axis=0, keepdims=True)),
            sign(jnp.sum(mix, axis=0, keepdims=True)) + mid_ref[0:1, :],
            mid_ref[1:2, :],
            mid_ref[2:3, :] + early_ref[...],
        ]
        out[...] = jnp.concatenate(rows + [jnp.zeros((TILE - 4, LANES), F32)], axis=0)

    return vmem_call(
        "post_grads", body, [((TILE, LANES), F32)], inputs=(mixed, cost_a, early, mid_part, *other)
    )[0]


def post_phase(shape, mixed, other, field_a):
    def body(own_ref, cos_a, sin_a, *refs):
        others, (psi_out, lam_out, token) = refs[:-3], refs[-3:]
        token[...] = jnp.zeros_like(token)
        first = lax.axis_index("core") == 0
        piece = shape.piece()
        slots = shape.slots()
        for start in range(0, shape.part, TILE):
            own_re, own_im = load_slots(shape, "all", [own_ref], start, slots)
            other_re, other_im = load_slots(shape, "other_part", others, start, slots)
            for i, slot in enumerate(slots):
                row = pl.multiple_of(piece(*slot) * shape.part + start, TILE)
                cosine, sine = cos_a[pl.ds(row, TILE), :], sin_a[pl.ds(row, TILE), :]
                own_pair = phased(own_re[i], own_im[i], cosine, sine)
                other_pair = phased(other_re[i], other_im[i], cosine, sine)
                for j in range(2):
                    span = pl.ds(2 * row + j, TILE, stride=2)
                    psi_out[span, :] = jnp.where(first, own_pair[j], other_pair[j])
                    lam_out[span, :] = jnp.where(first, other_pair[j], own_pair[j])

    return vmem_call(
        "post_phase",
        body,
        [shape.whole()] * 2 + [((TILE, LANES), F32)],
        inputs=(mixed, field_a[1], field_a[2], *other),
    )


AXES = ("grp", "z", "core")


def swap_cores(array):
    return lax.ppermute(array, "core", [(0, 1), (1, 0)])


def swap(shape, arrays, form):
    size = shape.depth
    out = list(arrays)
    with jax.named_scope("exchange_" + form):
        for i in sorted(range(1, size), key=lambda i: (i > 1, i.bit_count() == 1, -i)):
            pairs = []
            for chip in range(size * size):
                for core in range(CORES):
                    step = i if (core == 0) == (form == "u") else i * size
                    pairs.append((chip * CORES + core, (chip ^ step) * CORES + core))
            out[i] = lax.ppermute(arrays[i], AXES, pairs)
    return out


def join_grads(parts):
    def join(early, mid_part, late, out):
        rows = [late[0:1, :], late[1:2, :] + mid_part[0:1, :], mid_part[1:2, :], mid_part[2:3, :] + early[...]]
        out[...] = jnp.concatenate(rows + [jnp.zeros((TILE - 4, LANES), F32)], axis=0)

    return vmem_call("join_grads", join, [((TILE, LANES), F32)], inputs=tuple(parts))[0]


def total_grads(shape, block, token=None):
    def add(*refs):
        values = [ref[...] for ref in refs[:-1]]
        while len(values) > 1:
            values = [left + right for left, right in zip(values[::2], values[1::2])]
        refs[-1][...] = values[0]

    block_shape = [((TILE, LANES), F32)]
    for axis, size, most in (("core", CORES, 2), ("grp", shape.groups, 4), ("z", shape.depth, 4)):
        stride = 1
        while stride < size:
            reach = min(most, size // stride)
            others = [
                lax.ppermute(block, axis, [(j, j ^ (stride * i)) for j in range(size)]) for i in range(1, reach)
            ]
            last = axis == "z" and stride * reach == size and token is not None
            hold = (token,) if last else ()
            block = vmem_call("add_grads", add, block_shape, inputs=(block, *others), hold=hold)[0]
            stride *= reach
    scale = 2.0 / (shape.rows * LANES * shape.devices)

    def finish(ref, out):
        summed = jnp.sum(ref[...], axis=1, keepdims=True) * scale
        for i in range(2 * LAYERS):
            out[i] = jnp.sum(summed[i : i + 1, :])

    return vmem_call("finish_grads", finish, [((2 * LAYERS,), F32)], inputs=(block,), smem_out=True)[0]


def after(values, first):
    return lax.optimization_barrier((values, first))[0]


def piece_mix(shape, angles, which, state):
    low = shape.low
    least = shape.part.bit_length() - 1

    def body(angle, ref, mixed, flipped):
        sine, cosine = half_angle(angle[0:1, which : which + 1])
        real, imag = mixer_mats(low, cosine, sine, least)
        row_high, row_low = split(jnp.concatenate([real, imag], axis=0))
        row_flip = flip_mat(low, least)
        blocks = [ref[i * low : (i + 1) * low, :] for i in range(shape.planes)]
        for i, (re, im) in enumerate(rotate_all(blocks, None, None, row_high, row_low, cosine, sine)):
            mixed[i * low : (i + 1) * low, :LANES] = re
            mixed[i * low : (i + 1) * low, LANES:] = im
        for i, block in enumerate(flips_all(blocks, None, row_flip)):
            flipped[i * low : (i + 1) * low, :] = block

    return vmem_call(
        "piece_mix",
        body, [((shape.rows, 2 * LANES), F32)] * 2, inputs=(angles, state,)
    )


def plain_cross(lam, other):
    def body(lam_ref, other_ref, out):
        out[...] = cross_imag(lam_ref[...], other_ref[...])

    return vmem_call("plain_cross", body, [((1, LANES), F32)], inputs=(lam, other))[0]


def plain_gradients(shape, field_b, psi_before, lam_before):
    low = shape.low

    def body(cost, cos_b, sin_b, psi_ref, lam_ref, out):
        lane_flip, row_flip = flip_mats(low)
        spans = [slice(i * low, (i + 1) * low) for i in range(shape.planes)]
        psi = [psi_ref[span, :] for span in spans]
        lam = [lam_ref[span, :] for span in spans]
        inter = jnp.zeros((1, LANES), F32)
        mix_one = jnp.zeros((1, LANES), F32)
        mix_zero = jnp.zeros((1, LANES), F32)
        for i, flips in enumerate(flips_all(psi, lane_flip, row_flip)):
            mix_one = mix_one + cross_imag(lam[i], flips)
            inter = inter + cross_imag(lam[i], jnp.concatenate([cost[spans[i], :]] * 2, axis=1) * psi[i])

        def turned(block, span):
            re, im = phased(block[:, :LANES], block[:, LANES:], cos_b[span, :], sin_b[span, :])
            return jnp.concatenate([re, im], axis=1)

        psi = [turned(block, span) for block, span in zip(psi, spans)]
        for i, flips in enumerate(flips_all(psi, lane_flip, row_flip)):
            mix_zero = mix_zero + cross_imag(turned(lam[i], spans[i]), flips)
        out[...] = jnp.concatenate([mix_zero, inter, mix_one], axis=0)

    return vmem_call("plain_gradients", body, [((3, LANES), F32)], inputs=tuple(field_b) + (psi_before, lam_before))[0]


def plain_phase(shape, state, field, gradient):
    def body(ref, cost, cosine, sine, out):
        real, imag = ref[:, :LANES], ref[:, LANES:]
        if gradient:
            re, im = cost[...] * real, cost[...] * imag
        else:
            re, im = phased(real, imag, cosine[...], sine[...])
        out[:, :LANES] = re
        out[:, LANES:] = im

    return vmem_call("plain_phase", body, [((shape.rows, 2 * LANES), F32)], inputs=(state,) + tuple(field))[0]


def mid_math(shape, angles, planes, mats, cos_b, sin_b):
    low = shape.low
    sine, cosine = half_angle(angles[0:1, 3:4])
    first = rotate_all(planes, *[m[...] for m in mats[4:8]], cosine, sine)
    turned = []
    for i, (re, im) in enumerate(first):
        re, im = phased(re, im, cos_b[i * low : (i + 1) * low, :], sin_b[i * low : (i + 1) * low, :])
        turned.append(jnp.concatenate([re, im], axis=1))
    sine, cosine = half_angle(angles[0:1, 1:2])
    second = rotate_all(turned, *[m[...] for m in mats[0:4]], cosine, sine)
    return first, second


def plain_mid(shape, angles, state, field_b, mats):
    low = shape.low

    def body(angle, ref, cos_b, sin_b, *rest):
        blocks = [ref[i * low : (i + 1) * low, :] for i in range(shape.planes)]
        for out, pairs in zip(rest[8:], mid_math(shape, angle, blocks, rest[:8], cos_b, sin_b)):
            for i, (re, im) in enumerate(pairs):
                out[i * low : (i + 1) * low, :LANES] = re
                out[i * low : (i + 1) * low, LANES:] = im

    return vmem_call(
        "plain_mid",
        body,
        [((shape.rows, 2 * LANES), F32)] * 2,
        inputs=(angles, state, field_b[1], field_b[2]) + tuple(mats[0]) + tuple(mats[1]),
    )


def exchange_all(shape, state):
    block = state.reshape(shape.devices, -1, 2 * LANES)
    return lax.all_to_all(block, AXES, 0, 0, tiled=True).reshape(state.shape)


def plain(shape, forward, adjoint, edges, weights, layout, slab_bits, angles):
    rows = shape.rows

    def wide(array):
        return array.reshape(2, rows, LANES).transpose(1, 0, 2).reshape(rows, 2 * LANES)

    def narrow(array):
        return array.reshape(rows, 2, LANES).transpose(1, 0, 2).reshape(2, rows * LANES)

    def before(row):
        return shape.own() * rows + row

    def beyond(row):
        return (row // shape.part) * rows + shape.own() * shape.part + row % shape.part

    angles = angles.reshape(1, -1)
    small = small_inputs(edges, weights, layout, slab_bits)
    fields = make_fields(angles, *small, (rows, rows), before, beyond, shape.known)
    field_a, field_b = fields[:3], fields[3:]
    mats = make_mats(angles, shape.low)
    psi, flips = piece_mix(shape, angles, 3, wide(forward))
    lam, _ = piece_mix(shape, angles, 3, wide(adjoint))
    early = plain_cross(wide(adjoint), flips)
    psi_before, psi_after = plain_mid(shape, angles, exchange_all(shape, psi), field_b, mats)
    lam_before, lam_after = plain_mid(shape, angles, exchange_all(shape, lam), field_b, mats)
    mid_part = plain_gradients(shape, field_b, psi_before, lam_before)
    psi, lam = exchange_all(shape, psi_after), exchange_all(shape, lam_after)
    psi_mixed, flips = piece_mix(shape, angles, 1, psi)
    lam_mixed, _ = piece_mix(shape, angles, 1, lam)
    late = jnp.concatenate(
        [plain_cross(lam_mixed, plain_phase(shape, psi_mixed, field_a, True)), plain_cross(lam, flips)], axis=0
    )
    grads = total_grads(shape, join_grads((early, mid_part, late)))
    outs = [narrow(plain_phase(shape, state, field_a, False)) for state in (psi_mixed, lam_mixed)]
    return outs[0], outs[1], grads


def interleave(array, rows):
    return array.reshape(2, rows, LANES).transpose(1, 0, 2).reshape(2 * rows, LANES)


def deinterleave(array, rows):
    return array.reshape(rows, 2, LANES).transpose(1, 0, 2).reshape(2, rows * LANES)


def places(shape):
    def before(row):
        return shape.own() * shape.rows + row

    def beyond(row):
        far, slot, inner = row // shape.rows, (row % shape.rows) // shape.part, row % shape.part
        source = shape.piece()(slot // shape.depth, slot % shape.depth) * CORES
        source = source + jnp.bitwise_xor(lax.axis_index("core"), far)
        return source * shape.rows + shape.chip() * shape.part + inner

    return before, beyond


def pipelined(shape, forward, adjoint, edges, weights, layout, slab_bits, angles):
    rows = shape.rows
    angles = angles.reshape(1, -1)
    own_raw, other_raw, near = pre_near(shape, angles, interleave(forward, rows), interleave(adjoint, rows))
    far_raw = swap_cores(other_raw)
    mats = make_mats(angles, shape.low, hold=near[:1])
    before, beyond = places(shape)
    small = small_inputs(edges, weights, layout, slab_bits)
    sizes = (rows, 2 * rows), before, beyond, shape.known
    fields = make_fields(angles, *small, *sizes, core=1, hold=near[:1])
    near = swap(shape, near, "u")
    far = swap(shape, pre_far(shape, angles, far_raw), "u")
    near = swap(shape, rotate_local(shape, angles, near, "u", "v", mats[1], 3, hold=fields[:1]), "v")
    far = rotate_local(shape, angles, far, "u", "v", mats[1], 3)
    fields = make_fields(angles, *small, *sizes, core=0, hold=after(fields, far[0]))
    field_a, field_b = fields[:3], fields[3:]
    early = flip_raw(shape, own_raw, other_raw, hold=far[:1])
    far = swap(shape, far, "v")
    own_before, near, far = turn(shape, angles, near, far, field_b)
    far = swap(shape, far, "v")
    near = swap(shape, near, "v")
    other_before = swap_cores(own_before)
    far = swap(shape, rotate_local(shape, angles, far, "v", "u", mats[0], 1, hold=(other_before,)), "u")
    near = rotate_local(shape, angles, near, "v", "u", mats[0], 1)
    mid_part = gradients_mid(shape, field_b, own_before, other_before)
    other = [swap_cores(array) for array in post_send(shape, angles, far, hold=(near[0], mid_part, early))]
    near = swap(shape, near, "u")
    mixed = post_mix(shape, angles, near, hold=(mid_part, early))
    block = post_grads(shape, mixed, other, field_a[0], early, mid_part)
    psi_out, lam_out, token = post_phase(shape, mixed, other, field_a)
    grads = total_grads(shape, block, token)
    return deinterleave(psi_out, rows), deinterleave(lam_out, rows), grads


def solution(mesh):
    groups, rest = mesh.shape["grp"], mesh.shape["rep"]
    depth = rest // CORES
    fine = Mesh(mesh.devices.reshape(groups, depth, CORES), AXES)

    def per_device(forward, *others):
        shape = Shape(groups, depth, forward.shape[1])
        return (pipelined if shape.tiles else plain)(shape, forward, *others)

    state = P(None, AXES)
    return jax.shard_map(
        per_device,
        mesh=fine,
        in_specs=(state, state, P(), P(), P(), P(), P()),
        out_specs=(state, state, P()),
        check_vma=False,
    )
```
